256 devices in a mesh: replica: 32 (over z, y), tensor: 8 (over x, core).
Axes of the slice: x: 4, y: 4, z: 8, core: 2. Of those that a mesh axis runs over, the one named last changes fastest.
Arguments:
- hidden: bfloat16 [8192, 8192], P('replica'), may hold values from -6 to 6
- key_value_weight: bfloat16 [8192, 2, 1024], P(None, None, 'tensor'), may hold values from -0.0625 to 0.0625
- adapter_down_weight: bfloat16 [128, 8192, 128], P('replica', 'tensor'), may hold values from -0.0625 to 0.0625
- adapter_up_weight: bfloat16 [128, 2, 64, 1024], P('replica', None, None, 'tensor'), may hold values from -0.75 to 0.75
- token_adapter_index: int32 [8192], P('replica'), may hold values from 0 to 127, as said below
- destinations: int32 [8192, 1], P('replica'), may hold values from 0 to 31; in each aligned block of 256 rows (0 to 255, 256 to 511, ...) at most 16 rows name the same one
Outputs:
- kv_cache: bfloat16 [16384, 2, 1024], P('replica', None, 'tensor')
The draws below stay inside these ranges and needn't reach their ends.
Inputs may be any that keep to these rules, and one draw needn't show every extreme that they name: `token_adapter_index`: adapter a is stored on replica a // 4. The tokens arriving on one replica use exactly 8 distinct adapters, no two of them stored on the same replica. `destinations`: among the tokens arriving on one replica at most 16 have the same destination.
All inputs are finite; a program needn't handle non-finite values.
Results may differ from the reference program's by a relative error of at most 0.0029.
Values may be sent and summed in bfloat16 or wider, within the bound.
A program may use at most 128 MiB of HBM per device.

```python
import math
import jax
import jax.numpy as jnp
import numpy as np
from jax import lax

MODEL_DIM = 8192
KEY_VALUE_HEADS = 8
HEAD_SIZE = 128
ADAPTER_RANK = 64
TOK_DEV = 256
ADP_DEV = 4
USE = 8
CAP = 16
TOKENS = 8192
ADAPTER_COUNT = 128
N_REPLICA = 32


def draw_token_adapter_index(key, part):
    key = jax.random.fold_in(key, 7)
    owner_key, pick_key, slot_key, order_key = jax.random.split(key, 4)
    owner_keys = jax.random.split(owner_key, N_REPLICA)
    owners = jax.vmap(lambda sub_key: jax.random.permutation(sub_key, N_REPLICA)[:USE])(owner_keys)
    pick_local = jax.random.randint(pick_key, (N_REPLICA, USE), 0, ADP_DEV)
    chosen = owners * ADP_DEV + pick_local
    raw_draws = jax.random.randint(slot_key, (3, N_REPLICA, TOK_DEV), 0, USE)
    skewed = jnp.min(raw_draws, axis=0)
    forced = jnp.arange(TOK_DEV)[None, :]
    slot_table = jnp.where(forced < USE, forced, skewed)
    order_keys = jax.random.split(order_key, N_REPLICA)
    row_order = jax.vmap(lambda sub_key: jax.random.permutation(sub_key, TOK_DEV))(order_keys)
    slot_table = jnp.take_along_axis(slot_table, row_order, axis=1)
    adapter_table = jnp.take_along_axis(chosen, slot_table, axis=1)
    return adapter_table.reshape(N_REPLICA * TOK_DEV).astype(jnp.int32)


def shard_levels(own_key, extent, cuts, least, top_value):
    level, own = 1.0, jax.random.fold_in(own_key, 6)
    for position, blocks in cuts:
        heights = jnp.exp(jax.random.uniform(jax.random.fold_in(own, position), (blocks,), jnp.float32, least / len(cuts), top_value / len(cuts)))
        level = level * jnp.repeat(heights, extent[position] // blocks).reshape([-1 if axis == position else 1 for axis in range(len(extent))])
    return level


def shared_out(key, own, number, rows, count, top, reach, slope):
    ranking = jax.random.permutation(key, count)
    crowded, ordinary = load_shares(count, rows * top, reach, slope, True), load_shares(count, rows * top, reach, slope, False)
    places = jnp.arange(count)

    def named(tallies, turn):
        used = int((tallies > 0).sum())
        fixed = max(1, used // 4)
        moved = fixed + (places - fixed + turn * (used - fixed)) % max(1, count - fixed)
        return jnp.zeros((count,), jnp.int32).at[ranking[jnp.where(places < fixed, places, moved)]].set(jnp.asarray(tallies, jnp.int32))

    tallies = jnp.where(number % 4 == 0, named(crowded, number // 4), named(ordinary, number - number // 4 - 1))
    mixed = jax.random.permutation(jax.random.fold_in(own, 3), count)
    donor, sink = mixed[0:count // 2 * 2:2], mixed[1:count // 2 * 2:2]
    room = jnp.minimum(tallies[donor] - 1, reach - tallies[sink]) // 2
    room = jnp.where((donor == ranking[0]) | (sink == ranking[0]) | (tallies[sink] == 0), 0, jnp.maximum(room, 0))
    moved = jax.random.randint(jax.random.fold_in(own, 4), (count // 2,), 0, 1 << 20) % (room + 1)
    tallies = tallies.at[donor].add(-moved).at[sink].add(moved)
    items = jnp.searchsorted(jnp.cumsum(tallies), jnp.arange(rows * top), side="right").astype(jnp.int32)
    listing = items.reshape(top, rows).T
    listing = listing[jax.random.permutation(jax.random.fold_in(own, 1), rows)]
    turn = jax.random.randint(jax.random.fold_in(own, 2), (rows, 1), 0, top)
    return jnp.take_along_axis(listing, (jnp.arange(top)[None, :] + turn) % top, axis=1)


def load_shares(number_of, total, reach, skew, full):
    loads = [(1 << 20) // math.isqrt(standing ** skew) + 1 for standing in range(1, number_of + 1)]
    largest = reach if full else min(reach, max(-(-total // number_of), total * loads[0] // sum(loads)))
    least = 1 if total - largest >= number_of - 1 else 0
    given, spare = [largest] + [least] * (number_of - 1), total - largest - least * (number_of - 1)
    while spare > 0:
        movable = [i for i in range(1, number_of) if given[i] < largest] or [i for i in range(1, number_of) if given[i] < reach]
        pool, left = sum([loads[i] for i in movable]), spare
        for i in movable:
            addition = min(reach - given[i], max(1, left * loads[i] // pool), spare)
            given[i] = given[i] + addition
            spare = spare - addition
    return np.array(given)


def noise(rng, shape, scale, reach, shards=(), dtype=jnp.bfloat16):
    values = scale * jax.random.normal(rng, shape, jnp.float32)
    if shards:
        values = values * shard_levels(rng, shape, shards, -0.22, 0.18)
    return jnp.clip(values, -reach, reach).astype(dtype)


def setup_inputs(seed: int = 0) -> dict:
    seeds = jax.random.split(jax.random.key(seed), 7)
    hidden = noise(seeds[0], (TOKENS, MODEL_DIM), 1.0, 6.0, ((0, 32),))
    key_value_weight = noise(seeds[1], (MODEL_DIM, 2, KEY_VALUE_HEADS * HEAD_SIZE), MODEL_DIM ** -0.5, 0.0625, ((2, 8),))
    adapter_down_weight = noise(seeds[2], (ADAPTER_COUNT, MODEL_DIM, 2 * ADAPTER_RANK), MODEL_DIM ** -0.5, 0.0625, ((0, 32), (1, 8)))
    adapter_up_weight = noise(seeds[3], (ADAPTER_COUNT, 2, ADAPTER_RANK, KEY_VALUE_HEADS * HEAD_SIZE), ADAPTER_RANK ** -0.5, 0.75, ((0, 32), (3, 8)))
    token_adapter_index = draw_token_adapter_index(jax.random.fold_in(seeds[6], 71), 0)
    destinations_keys = jax.random.split(jax.random.fold_in(seeds[5], 1), TOKENS // TOK_DEV)
    destinations_turns = jax.random.permutation(jax.random.fold_in(seeds[5], 3), TOKENS // TOK_DEV)
    destinations = jax.vmap(lambda own, number: shared_out(jax.random.fold_in(seeds[5], 2), own, number, TOK_DEV, N_REPLICA, 1, CAP, 2))(destinations_keys, destinations_turns).reshape((TOKENS, 1))
    return {"hidden": hidden, "key_value_weight": key_value_weight, "adapter_down_weight": adapter_down_weight, "adapter_up_weight": adapter_up_weight, "token_adapter_index": token_adapter_index, "destinations": destinations}


adapter_scale = 0.5


def reference(hidden, key_value_weight, adapter_down_weight, adapter_up_weight, token_adapter_index, destinations):
    token_count = hidden.shape[0]
    head_cols = key_value_weight.shape[2]
    base_projection = jnp.dot(hidden, key_value_weight.reshape(MODEL_DIM, 2 * head_cols), preferred_element_type=jnp.float32)
    base_projection = base_projection.reshape(token_count, 2, head_cols)
    group_rows = 8
    grouped_rows = hidden.reshape(token_count // group_rows, group_rows, MODEL_DIM)
    adapter_index_groups = token_adapter_index.reshape(token_count // group_rows, group_rows)

    def adapter_row_values(carried_state, loop_element):
        row_block, chosen_adapter_index = loop_element
        down_weight_rows = jnp.take(adapter_down_weight, chosen_adapter_index, axis=0).astype(jnp.float32)
        shrink = jnp.einsum("nd,ndr->nr", row_block.astype(jnp.float32), down_weight_rows).astype(jnp.bfloat16)
        shrink = lax.optimization_barrier(shrink).astype(jnp.float32)
        up_weight_rows = jnp.take(adapter_up_weight, chosen_adapter_index, axis=0).astype(jnp.float32)
        rank_pairs = shrink.reshape(group_rows, 2, ADAPTER_RANK)
        delta_block = jnp.einsum("npr,nprc->npc", rank_pairs, up_weight_rows)
        return carried_state, delta_block

    closing_state, every_update = lax.scan(adapter_row_values, jnp.float32(0.0), (grouped_rows, adapter_index_groups))
    every_update = every_update.reshape(token_count, 2, head_cols)
    projected_output = (base_projection + adapter_scale * every_update).astype(jnp.bfloat16)
    dest_table = destinations[:, 0].astype(jnp.int32).reshape(N_REPLICA, TOK_DEV)
    replica_ids = jnp.arange(N_REPLICA).astype(jnp.int32)
    dest_onehot = (dest_table[:, :, None] == replica_ids[None, None, :]).astype(jnp.int32)
    dest_order = jnp.sum((jnp.cumsum(dest_onehot, axis=1) - 1) * dest_onehot, axis=2)
    source_rank = replica_ids[:, None]
    target_rows = ((dest_table * N_REPLICA + source_rank) * CAP + dest_order).astype(jnp.int32)
    kv_rows = jnp.zeros((N_REPLICA * N_REPLICA * CAP, 2, head_cols), jnp.bfloat16)
    return kv_rows.at[target_rows.reshape(-1)].set(projected_output)
```

```python
import functools

import jax
import jax.numpy as jnp
from jax import lax
from jax.experimental import pallas as pl
from jax.experimental.pallas import tpu as pltpu
from jax.sharding import PartitionSpec as P

RINGS = 8
USE = 8
SCALE = 0.5
CHUNKS = 4

BF16 = jnp.bfloat16
F32 = jnp.float32
MESH = pl.DeviceIdType.MESH


def slot_of(d, n):
    d %= n
    return 0 if d == 0 else (2 * d - 1 if d <= n // 2 else 2 * (n - d))


def shift_of(k, n):
    odd = k % 2
    return odd * ((k + 1) // 2) + (1 - odd) * ((n - k // 2) % n)


def kernel(
    dims,
    hid, kvw, down, up, idx, dest,
    out,
    hf, kvb, kvf, base, hbuf, wbuf, upz, colbuf, idz, idy, acc, rs, sh, hm, sr, upsend, upsel, bd, perm, kvs,
    local_sem, z_send, z_recv, w_send, w_recv, u_send, u_recv, i_send, i_recv, j_send, j_recv,
    a_send, a_recv, b_send, b_recv, c_send, c_recv, s_send, s_recv, o_send, o_recv,
):
    nz, ny, nt = dims
    rows, width = hbuf.shape[1], hbuf.shape[2]
    adapters, rank = wbuf.shape[1], wbuf.shape[3]
    sub = rows // nt
    piece = rows // CHUNKS
    cap2 = kvs.shape[1]
    replicas = nz * ny
    hz, hy = nz // 2, ny // 2

    r = lax.axis_index("replica")
    t = lax.axis_index("tensor")
    z, y = r // ny, r % ny

    def at_z(d):
        return ((z + d + nz) % nz) * ny + y

    def at_y(d):
        return z * ny + (y + d + ny) % ny

    def remote(src, dst, send, recv, replica, tensor):
        return pltpu.make_async_remote_copy(
            src_ref=src, dst_ref=dst, send_sem=send, recv_sem=recv,
            device_id=(replica, tensor), device_id_type=MESH,
        )

    own_cols = pl.ds(pl.multiple_of(t * width, 128), width)
    own_h = pltpu.make_async_copy(hid.at[:, own_cols], hbuf.at[0], local_sem.at[0])
    own_w = pltpu.make_async_copy(down, wbuf.at[0], local_sem.at[1])
    own_u = pltpu.make_async_copy(up, upz.at[0], local_sem.at[2])
    own_k = pltpu.make_async_copy(kvw, kvb, local_sem.at[3])

    def full_copy(c):
        return pltpu.make_async_copy(
            hid.at[:, pl.ds(pl.multiple_of(c * width, 128), width)], hf.at[c], local_sem.at[4 + c]
        )

    own_h.start()
    own_w.start()
    own_u.start()
    own_k.start()
    lax.fori_loop(0, nt, lambda c, _: (full_copy(c).start(), 0)[1], 0)

    barrier = pltpu.get_barrier_semaphore()

    def greet_replica(i, _):
        pl.semaphore_signal(
            barrier, inc=1, device_id=((r + i) % replicas, t), device_id_type=MESH
        )
        return 0

    def greet_tensor(i, _):
        pl.semaphore_signal(barrier, inc=1, device_id=(r, (t + i) % nt), device_id_type=MESH)
        return 0

    lax.fori_loop(1, replicas, greet_replica, 0)
    lax.fori_loop(1, nt, greet_tensor, 0)
    pl.semaphore_wait(barrier, replicas - 1 + nt - 1)

    def z_copy(way, step, c):
        part = pl.ds(c * piece, piece)
        sign = -1 if way == 0 else 1
        to = at_z(1 if way == 0 else -1)
        dst = hbuf.at[slot_of(sign * step, nz), part]
        if step == 1:
            src = hid.at[part, own_cols]
        else:
            src = hbuf.at[slot_of(sign * (step - 1), nz), part]
        return remote(src, dst, z_send.at[way, step, c], z_recv.at[way, step, c], to, t)

    def z_takes(way, step, c):
        return step < hz or (step == hz and (c < CHUNKS // 2) == (way == 0))

    def u_copy(way, step):
        sign = -1 if way == 0 else 1
        to = at_z(1 if way == 0 else -1)
        n = upz.shape[1]
        part = pl.ds(0, n) if step < hz else pl.ds(way * (n // 2), n // 2)
        dst = upz.at[slot_of(sign * step, nz), part]
        if step == 1:
            src = up.at[part]
        else:
            src = upz.at[slot_of(sign * (step - 1), nz), part]
        return remote(src, dst, u_send.at[way, step], u_recv.at[way, step], to, t)

    def w_copy(way, step, j):
        sign = -1 if way == 0 else 1
        to = at_y(1 if way == 0 else -1)
        dst = wbuf.at[slot_of(sign * step, ny), j]
        src = down.at[j] if step == 1 else wbuf.at[slot_of(sign * (step - 1), ny), j]
        return remote(src, dst, w_send.at[way, step, j], w_recv.at[way, step, j], to, t)

    def w_takes(way, step, j):
        return step < hy or (step == hy and (j < adapters // 2) == (way == 0))

    def i_copy(d):
        return remote(idx, idz.at[slot_of(-d, nz)], i_send.at[d], i_recv.at[d], at_z(d), t)

    def j_copy(d):
        return remote(idx, idy.at[(-d) % ny], j_send.at[d], j_recv.at[d], at_y(d), t)

    for d in range(1, nz):
        i_copy(d).start()
    for d in range(1, ny):
        j_copy(d).start()
    w_order = [list(range(adapters)), list(range(adapters // 2, adapters)) + list(range(adapters // 2))]
    for c in range(CHUNKS):
        for way in range(2):
            if z_takes(way, 1, c):
                z_copy(way, 1, c).start()
        for way in range(2):
            if c < adapters and w_takes(way, 1, w_order[way][c]):
                w_copy(way, 1, w_order[way][c]).start()
    for way in range(2):
        u_copy(way, 1).start()

    eye = lax.broadcasted_iota(jnp.int32, (rows, rows), 0) == lax.broadcasted_iota(
        jnp.int32, (rows, rows), 1
    )

    def column(row):
        wide = jnp.broadcast_to(row, (rows, rows))
        return jnp.sum(jnp.where(eye, wide, 0.0), axis=1, keepdims=True)

    def base_part(c, _):
        words = 2 * width
        at = pl.ds(pl.multiple_of(c * words, 128), words)
        kvf[...] = kvb[at, :].astype(F32)
        keys = kvf[pl.ds(0, width, stride=2), :].astype(BF16)
        values = kvf[pl.ds(1, width, stride=2), :].astype(BF16)
        both = jnp.concatenate([keys, values], axis=1)
        base[...] += jnp.dot(hf[c], both, preferred_element_type=F32)
        return 0

    def unit(k, m):
        mate = shift_of(m, ny)
        first = (z * ny + (y + mate) % ny) * adapters
        wanted = colbuf[k]
        total = acc[k].reshape(rows, rank)
        h = hbuf[k]
        for pair in range(adapters // 2):
            w = jnp.concatenate([wbuf[m, 2 * pair], wbuf[m, 2 * pair + 1]], axis=1)
            got = jnp.dot(h, w, preferred_element_type=F32)
            for j in range(2):
                mine = wanted == first + 2 * pair + j
                total = total + jnp.where(mine, got[:, j * rank : (j + 1) * rank], 0.0)
        acc[k] = total.reshape(nt, sub, rank)

    def units(k_low, k_high, m_low, m_high):
        count = m_high - m_low

        def one(i, _):
            unit(k_low + i // count, m_low + i % count)
            return 0

        lax.fori_loop(0, (k_high - k_low) * count, one, 0)

    base[...] = jnp.zeros_like(base)
    acc[...] = jnp.zeros_like(acc)
    to_row = dest[...].astype(F32)
    to_col = column(to_row)
    before = lax.broadcasted_iota(jnp.int32, (rows, rows), 0) < lax.broadcasted_iota(
        jnp.int32, (rows, rows), 1
    )
    earlier = jnp.where(before & (to_col == to_row), 1.0, 0.0)
    order = jnp.sum(earlier, axis=0, keepdims=True)
    place = to_row * float(cap2) + order * 2.0
    n_perm = perm.shape[0]
    for p in range(2):
        target = lax.broadcasted_iota(jnp.int32, (n_perm, rows), 0).astype(F32)
        perm[:, p * rows : (p + 1) * rows] = jnp.where(target == place + float(p), 1.0, 0.0).astype(
            BF16
        )

    def wide_column(k, row):
        colbuf[k] = jnp.broadcast_to(column(row.astype(F32)), (rows, rank)).astype(jnp.int32)

    wide_column(0, idx[...])
    own_h.wait()
    own_w.wait()
    own_k.wait()
    lax.fori_loop(0, nt, lambda c, _: (full_copy(c).wait(), 0)[1], 0)
    unit(0, 0)
    for d in range(1, nz):
        i_copy(d).wait_recv()
        k = slot_of(-d, nz)
        wide_column(k, idz[k])

    base_done = 0
    w_step1 = [(way, w_order[way][n]) for n in range(adapters) for way in range(2)]
    w_step1 = [(way, j) for way, j in w_step1 if w_takes(way, 1, j)]
    w_next = 0
    for step in range(1, hz):
        for c in range(CHUNKS):
            for way in range(2):
                z_copy(way, step, c).wait_recv()
                if z_takes(way, step + 1, c):
                    z_copy(way, step + 1, c).start()
            if c % 2 == 1:
                for _ in range(2):
                    if w_next < len(w_step1):
                        way, j = w_step1[w_next]
                        w_copy(way, 1, j).wait_recv()
                        if hy > 1 and w_takes(way, 2, j):
                            w_copy(way, 2, j).start()
                        w_next += 1
            if base_done < nt:
                more = min(2, nt - base_done)
                lax.fori_loop(base_done, base_done + more, base_part, 0)
                base_done += more
        for way in range(2):
            u_copy(way, step).wait_recv()
            u_copy(way, step + 1).start()
        if step == 1:
            units(1, 3, 0, 1)
        elif step == 2:
            units(3, 5, 0, 1)
    for way, j in w_step1[w_next:]:
        w_copy(way, 1, j).wait_recv()
        if hy > 1 and w_takes(way, 2, j):
            w_copy(way, 2, j).start()
    if base_done < nt:
        lax.fori_loop(base_done, nt, base_part, 0)
    early = min(nz - 1, 5)
    if hy > 1:
        units(0, early, 1, 3)
        for j in range(adapters):
            w_copy(0 if j < adapters // 2 else 1, 2, j).wait_recv()
    units(0, early, ny - 1, ny)
    if early < nz - 1:
        units(early, nz - 1, 0, ny)

    def a_copy(i, part, low, count):
        to = (t + i) % nt
        span = pl.ds(low, count)
        return remote(
            acc.at[span, to], rs.at[i, span], a_send.at[part, i], a_recv.at[part, i], r, to
        )

    def start_a(part, low, count):
        lax.fori_loop(1, nt, lambda i, _: (a_copy(i, part, low, count).start(), 0)[1], 0)

    def finish_a(part, low, count):
        lax.fori_loop(1, nt, lambda i, _: (a_copy(i, part, low, count).wait_recv(), 0)[1], 0)
        total = acc[low : low + count, t]
        for i in range(1, nt):
            total = total + rs[i, low : low + count]
        sh[low : low + count] = total.astype(BF16)

    def b_copy(k):
        d = 0 if k == 0 else next(d for d in range(1, nz) if slot_of(d, nz) == k)
        return remote(
            sh.at[k], hm.at[slot_of(-d, nz)], b_send.at[k], b_recv.at[slot_of(-d, nz)], at_z(d), t
        )

    start_a(0, 0, nz - 1)

    for way in range(2):
        u_copy(way, hz).wait_recv()
    own_u.wait()
    for d in range(1, ny):
        j_copy(d).wait_recv()

    def select_up(wanted, into):
        def one(k, _):
            first = (((z + shift_of(k, nz)) % nz) * ny + y) * adapters
            total = jnp.zeros((rank, 128), F32)
            for j in range(adapters):
                uses = jnp.where(wanted == first + j, 1.0, 0.0)
                uses = jnp.max(uses, axis=1, keepdims=True)
                total = total + uses * upz[k, j * rank : (j + 1) * rank].astype(F32)
            into[k] = total.astype(BF16)
            return 0

        lax.fori_loop(0, nz, one, 0)

    def s_copy(d):
        return remote(
            upsend.at[d], upsel.at[(-d) % ny], s_send.at[d], s_recv.at[d], at_y(d), t
        )

    for d in range(1, ny):
        select_up(idy[d], upsend.at[d])
        s_copy(d).start()
    select_up(idx[...], upsel.at[0])

    finish_a(0, 0, nz - 1)
    hm[0] = sh[0]
    for k in range(1, nz - 1):
        b_copy(k).start()
    for c in range(CHUNKS):
        way = 0 if c < CHUNKS // 2 else 1
        z_copy(way, hz, c).wait_recv()
    units(nz - 1, nz, 0, ny)
    start_a(1, nz - 1, 1)

    rank_half = (lax.broadcasted_iota(jnp.int32, (rank, 128), 0) < rank // 2).astype(F32)

    def spread_up(e):
        def one(k, _):
            block = upsel[e, k].astype(F32)
            bd[e, pl.ds(pl.multiple_of(k * rank, rank), rank), 0:128] = (block * rank_half).astype(BF16)
            bd[e, pl.ds(pl.multiple_of(k * rank, rank), rank), 128:256] = (
                block * (1.0 - rank_half)
            ).astype(BF16)
            return 0

        lax.fori_loop(0, nz, one, 0)

    spread_up(0)
    finish_a(1, nz - 1, 1)
    b_copy(nz - 1).start()
    for d in range(1, ny):
        s_copy(d).wait_recv()
        spread_up(ny - d)

    for k in range(1, nz):
        b_copy(k).wait_recv()
    mine = hm[0].astype(F32)
    for k in range(1, nz):
        mine = mine + hm[k].astype(F32)
    sr[t] = mine.astype(BF16)

    def c_copy(i):
        return remote(sr.at[t], sr.at[t], c_send.at[i], c_recv.at[i], r, (t + i) % nt)

    def c_arrival(i):
        src = (t + nt - i) % nt
        return remote(sr.at[src], sr.at[src], c_send.at[i], c_recv.at[i], r, src)

    lax.fori_loop(1, nt, lambda i, _: (c_copy(i).start(), 0)[1], 0)
    lax.fori_loop(1, nt, lambda i, _: (c_arrival(i).wait_recv(), 0)[1], 0)

    shrink = sr[...].astype(F32).reshape(rows, rank)
    wanted = colbuf[0]

    def delta_part(e, _):
        parts = []
        for k in range(nz):
            d = shift_of(k, nz)
            first = (((z + d) % nz) * ny + (y + e) % ny) * adapters
            uses = (wanted >= first) & (wanted < first + adapters)
            parts.append(jnp.where(uses, shrink, 0.0).astype(BF16))
        spread = jnp.concatenate(parts, axis=1)
        base[...] += SCALE * jnp.dot(spread, bd[e], preferred_element_type=F32)
        return 0

    lax.fori_loop(0, ny, delta_part, 0)
    projected = base[...].astype(BF16)
    stacked = jnp.concatenate([projected[:, 0:128], projected[:, 128:256]], axis=0)
    cache = jnp.dot(perm[...], stacked, preferred_element_type=F32).astype(BF16)
    kvs[...] = cache.reshape(replicas, cap2, 128)

    def o_copy(i):
        to = (r + i) % replicas
        return remote(
            kvs.at[to], out.at[pl.ds(pl.multiple_of(r * cap2, cap2), cap2)],
            o_send.at[i], o_recv.at[i], to, t,
        )

    def o_arrival(i):
        src = (r + replicas - i) % replicas
        return remote(
            kvs.at[src], out.at[pl.ds(pl.multiple_of(src * cap2, cap2), cap2)],
            o_send.at[i], o_recv.at[i], src, t,
        )

    lax.fori_loop(1, replicas, lambda i, _: (o_copy(i).start(), 0)[1], 0)
    own_o = pltpu.make_async_copy(
        kvs.at[r], out.at[pl.ds(pl.multiple_of(r * cap2, cap2), cap2)], local_sem.at[4 + nt]
    )
    own_o.start()

    for way in range(2):
        for step in range(1, hz + 1):
            for c in range(CHUNKS):
                if z_takes(way, step, c):
                    z_copy(way, step, c).wait_send()
            u_copy(way, step).wait_send()
        for step in range(1, hy + 1):
            for j in range(adapters):
                if w_takes(way, step, j):
                    w_copy(way, step, j).wait_send()
    for d in range(1, nz):
        i_copy(d).wait_send()
    for d in range(1, ny):
        j_copy(d).wait_send()
        s_copy(d).wait_send()
    for k in range(1, nz):
        b_copy(k).wait_send()

    def tensor_sends(i, _):
        a_copy(i, 0, 0, nz - 1).wait_send()
        a_copy(i, 1, nz - 1, 1).wait_send()
        c_copy(i).wait_send()
        return 0

    lax.fori_loop(1, nt, tensor_sends, 0)

    def last(i, _):
        o_copy(i).wait_send()
        o_arrival(i).wait_recv()
        return 0

    lax.fori_loop(1, replicas, last, 0)
    own_o.wait()


def shards(nz, hidden, key_value_weight, adapter_down_weight, adapter_up_weight, token_adapter_index, destinations):
    replicas = lax.axis_size("replica")
    nt = lax.axis_size("tensor")
    ny = replicas // nz
    rows, model = hidden.shape
    width = model // nt
    adapters, _, rank = adapter_down_weight.shape
    cols = key_value_weight.shape[2]
    cap2 = 2 * (2 * rows // replicas)
    sub = rows // nt
    hz, hy = nz // 2, ny // 2
    vm = pltpu.VMEM
    dma = pltpu.SemaphoreType.DMA
    scratch = [
        vm((nt, rows, width), BF16),
        vm((2 * model, cols), BF16),
        vm((2 * width, cols), F32),
        vm((rows, 2 * cols), F32),
        vm((nz, rows, width), BF16),
        vm((ny, adapters, width, rank), BF16),
        vm((nz, adapters * rank, cols), BF16),
        vm((nz, rows, rank), jnp.int32),
        vm((nz, 1, rows), jnp.int32),
        vm((ny, 1, rows), jnp.int32),
        vm((nz, nt, sub, rank), F32),
        vm((nt, nz, sub, rank), F32),
        vm((nz, sub, rank), BF16),
        vm((nz, sub, rank), BF16),
        vm((nt, sub, rank), BF16),
        vm((ny, nz, rank, cols), BF16),
        vm((ny, nz, rank, cols), BF16),
        vm((ny, nz * rank, 2 * cols), BF16),
        vm((replicas * cap2, 2 * rows), BF16),
        vm((replicas, cap2, cols), BF16),
        dma((5 + nt,)),
        dma((2, hz + 1, CHUNKS)), dma((2, hz + 1, CHUNKS)),
        dma((2, hy + 1, adapters)), dma((2, hy + 1, adapters)),
        dma((2, hz + 1)), dma((2, hz + 1)),
        dma((nz,)), dma((nz,)),
        dma((ny,)), dma((ny,)),
        dma((2, nt)), dma((2, nt)),
        dma((nz,)), dma((nz,)),
        dma((nt,)), dma((nt,)),
        dma((ny,)), dma((ny,)),
        dma((replicas,)), dma((replicas,)),
    ]
    hbm = pl.BlockSpec(memory_space=pltpu.HBM)
    in_vmem = pl.BlockSpec(memory_space=pltpu.VMEM)
    cache = pl.pallas_call(
        functools.partial(kernel, (nz, ny, nt)),
        out_shape=jax.ShapeDtypeStruct((replicas * cap2, cols), BF16),
        in_specs=[hbm, hbm, hbm, hbm, in_vmem, in_vmem],
        out_specs=hbm,
        scratch_shapes=scratch,
        compiler_params=pltpu.CompilerParams(
            collective_id=0, has_side_effects=True, vmem_limit_bytes=56 * 1024 * 1024
        ),
        cost_estimate=pl.CostEstimate(
            flops=2 * rows * model * 2 * cols + 2 * nz * rows * width * ny * adapters * rank,
            bytes_accessed=2 * (rows * model + 2 * model * cols + adapters * width * rank),
            transcendentals=0,
        ),
    )(
        hidden,
        key_value_weight.reshape(2 * model, cols),
        adapter_down_weight,
        adapter_up_weight.reshape(adapters * rank, cols),
        token_adapter_index.reshape(1, rows),
        destinations.reshape(1, rows),
    )
    return cache.reshape(replicas * cap2 // 2, 2, cols)


def solution(mesh):
    placed = (
        P("replica", None),
        P(None, None, "tensor"),
        P("replica", "tensor", None),
        P("replica", None, None, "tensor"),
        P("replica"),
        P("replica", None),
    )
    return jax.shard_map(
        functools.partial(shards, RINGS), mesh=mesh, in_specs=placed,
        out_specs=P("replica", None, "tensor"), check_vma=False,
    )
```

```python
import functools

import jax
import jax.numpy as jnp
from jax import lax
from jax.experimental import pallas as pl
from jax.experimental.pallas import tpu as pltpu
from jax.sharding import PartitionSpec as P

RINGS = 8
USE = 8
SCALE = 0.5
CHUNKS = 4

BF16 = jnp.bfloat16
F32 = jnp.float32
MESH = pl.DeviceIdType.MESH


def slot_of(d, n):
    d %= n
    return 0 if d == 0 else (2 * d - 1 if d <= n // 2 else 2 * (n - d))


def shift_of(k, n):
    odd = k % 2
    return odd * ((k + 1) // 2) + (1 - odd) * ((n - k // 2) % n)


def kernel(
    dims,
    hid, kvw, down, up, idx, dest,
    out,
    hf, kvb, kvf, base, hbuf, wbuf, upz, colbuf, idz, idy, acc, halves, part, rs, sh, hm, sr, upsend, upsel, bd, perm, kvs,
    local_sem, z_send, z_recv, w_send, w_recv, u_send, u_recv, i_send, i_recv, j_send, j_recv,
    p_send, p_recv, a_send, a_recv, b_send, b_recv, c_send, c_recv, s_send, s_recv, o_send, o_recv,
):
    nz, ny, nt = dims
    rows, width = hbuf.shape[1], hbuf.shape[2]
    adapters, rank = wbuf.shape[1], wbuf.shape[3]
    sub = rows // nt
    piece = rows // CHUNKS
    cap2 = kvs.shape[1]
    replicas = nz * ny
    hz, hy = nz // 2, ny // 2

    r = lax.axis_index("replica")
    t = lax.axis_index("tensor")
    z, y = r // ny, r % ny
    nx = nt // 2
    x, core = t // 2, t % 2
    share = core * nx + x

    def at_z(d):
        return ((z + d + nz) % nz) * ny + y

    def at_y(d):
        return z * ny + (y + d + ny) % ny

    def remote(src, dst, send, recv, replica, tensor):
        return pltpu.make_async_remote_copy(
            src_ref=src, dst_ref=dst, send_sem=send, recv_sem=recv,
            device_id=(replica, tensor), device_id_type=MESH,
        )

    own_cols = pl.ds(pl.multiple_of(t * width, 128), width)
    own_h = pltpu.make_async_copy(hid.at[:, own_cols], hbuf.at[0], local_sem.at[0])
    own_w = pltpu.make_async_copy(down, wbuf.at[0], local_sem.at[1])
    own_u = pltpu.make_async_copy(up, upz.at[0], local_sem.at[2])
    own_k = pltpu.make_async_copy(kvw, kvb, local_sem.at[3])

    def full_copy(c):
        return pltpu.make_async_copy(
            hid.at[:, pl.ds(pl.multiple_of(c * width, 128), width)], hf.at[c], local_sem.at[4 + c]
        )

    own_h.start()
    own_w.start()
    own_u.start()
    own_k.start()
    lax.fori_loop(0, nt, lambda c, _: (full_copy(c).start(), 0)[1], 0)

    barrier = pltpu.get_barrier_semaphore()

    def greet_tensor(i, _):
        pl.semaphore_signal(barrier, inc=1, device_id=(r, (t + i) % nt), device_id_type=MESH)
        return 0

    for to in (at_z(1), at_z(-1), at_y(1), at_y(-1)):
        pl.semaphore_signal(barrier, inc=1, device_id=(to, t), device_id_type=MESH)
    lax.fori_loop(1, nt, greet_tensor, 0)
    pl.semaphore_wait(barrier, 4 + nt - 1)

    def z_copy(way, step, c):
        part = pl.ds(c * piece, piece)
        sign = -1 if way == 0 else 1
        to = at_z(1 if way == 0 else -1)
        dst = hbuf.at[slot_of(sign * step, nz), part]
        if step == 1:
            src = hid.at[part, own_cols]
        else:
            src = hbuf.at[slot_of(sign * (step - 1), nz), part]
        return remote(src, dst, z_send.at[way, step, c], z_recv.at[way, step, c], to, t)

    def z_takes(way, step, c):
        return step < hz or (step == hz and (c < CHUNKS // 2) == (way == 0))

    def u_copy(way, step, h):
        sign = -1 if way == 0 else 1
        to = at_z(1 if way == 0 else -1)
        n = upz.shape[1] // 2
        part = pl.ds(h * n, n)
        dst = upz.at[slot_of(sign * step, nz), part]
        if step == 1:
            src = up.at[part]
        else:
            src = upz.at[slot_of(sign * (step - 1), nz), part]
        return remote(src, dst, u_send.at[way, step, h], u_recv.at[way, step, h], to, t)

    def u_takes(way, step, h):
        return step < hz or (step == hz and h == way)

    def u_start():
        for h in range(2):
            for way in range(2):
                if u_takes(way, 1, h):
                    u_copy(way, 1, h).start()

    def w_copy(way, step, j):
        sign = -1 if way == 0 else 1
        to = at_y(1 if way == 0 else -1)
        dst = wbuf.at[slot_of(sign * step, ny), j]
        src = down.at[j] if step == 1 else wbuf.at[slot_of(sign * (step - 1), ny), j]
        return remote(src, dst, w_send.at[way, step, j], w_recv.at[way, step, j], to, t)

    def w_takes(way, step, j):
        return step < hy or (step == hy and (j < adapters // 2) == (way == 0))

    def i_copy(way, step):
        sign = -1 if way == 0 else 1
        src = idx if step == 1 else idz.at[slot_of(sign * (step - 1), nz)]
        dst = idz.at[slot_of(sign * step, nz)]
        to = at_z(1 if way == 0 else -1)
        return remote(src, dst, i_send.at[way, step], i_recv.at[way, step], to, t)

    def j_copy(way, step):
        sign = -1 if way == 0 else 1
        src = idx if step == 1 else idy.at[(sign * (step - 1)) % ny]
        dst = idy.at[(sign * step) % ny]
        to = at_y(1 if way == 0 else -1)
        return remote(src, dst, j_send.at[way, step], j_recv.at[way, step], to, t)

    def once(way, step, half_way):
        return step < half_way or (step == half_way and way == 0)

    for way in range(2):
        if once(way, 1, hz):
            i_copy(way, 1).start()
        if once(way, 1, hy):
            j_copy(way, 1).start()
    w_order = [list(range(adapters)), list(range(adapters // 2, adapters)) + list(range(adapters // 2))]
    for c in range(CHUNKS):
        for way in range(2):
            if z_takes(way, 1, c):
                z_copy(way, 1, c).start()
        for way in range(2):
            if c < adapters and w_takes(way, 1, w_order[way][c]):
                w_copy(way, 1, w_order[way][c]).start()
    u_start()

    eye = lax.broadcasted_iota(jnp.int32, (rows, rows), 0) == lax.broadcasted_iota(
        jnp.int32, (rows, rows), 1
    )

    def column(row):
        wide = jnp.broadcast_to(row, (rows, rows))
        return jnp.sum(jnp.where(eye, wide, 0.0), axis=1, keepdims=True)

    def base_part(c, _):
        words = 2 * width
        at = pl.ds(pl.multiple_of(c * words, 128), words)
        kvf[...] = kvb[at, :].astype(F32)
        keys = kvf[pl.ds(0, width, stride=2), :].astype(BF16)
        values = kvf[pl.ds(1, width, stride=2), :].astype(BF16)
        both = jnp.concatenate([keys, values], axis=1)
        base[...] += jnp.dot(hf[c], both, preferred_element_type=F32)
        return 0

    def unit(k, m):
        mate = shift_of(m, ny)
        first = (z * ny + (y + mate) % ny) * adapters
        wanted = colbuf[k]
        total = acc[k].reshape(rows, rank)
        h = hbuf[k]
        for pair in range(adapters // 2):
            w = jnp.concatenate([wbuf[m, 2 * pair], wbuf[m, 2 * pair + 1]], axis=1)
            got = jnp.dot(h, w, preferred_element_type=F32)
            for j in range(2):
                mine = wanted == first + 2 * pair + j
                total = total + jnp.where(mine, got[:, j * rank : (j + 1) * rank], 0.0)
        acc[k] = total.reshape(2, nx, sub, rank)

    def units(k_low, k_high, m_low, m_high):
        count = m_high - m_low

        def one(i, _):
            unit(k_low + i // count, m_low + i % count)
            return 0

        if (k_high - k_low) * count == 1:
            unit(k_low, m_low)
        else:
            lax.fori_loop(0, (k_high - k_low) * count, one, 0)

    base[...] = jnp.zeros_like(base)
    acc[...] = jnp.zeros_like(acc)
    to_row = dest[...].astype(F32)
    to_col = column(to_row)
    before = lax.broadcasted_iota(jnp.int32, (rows, rows), 0) < lax.broadcasted_iota(
        jnp.int32, (rows, rows), 1
    )
    earlier = jnp.where(before & (to_col == to_row), 1.0, 0.0)
    order = jnp.sum(earlier, axis=0, keepdims=True)
    place = to_row * float(cap2) + order * 2.0
    n_perm = perm.shape[0]
    for p in range(2):
        target = lax.broadcasted_iota(jnp.int32, (n_perm, rows), 0).astype(F32)
        perm[:, p * rows : (p + 1) * rows] = jnp.where(target == place + float(p), 1.0, 0.0).astype(
            BF16
        )

    def wide_column(k, row):
        colbuf[k] = jnp.broadcast_to(column(row.astype(F32)), (rows, rank)).astype(jnp.int32)

    wide_column(0, idx[...])
    own_h.wait()
    own_w.wait()
    own_k.wait()
    lax.fori_loop(0, nt, lambda c, _: (full_copy(c).wait(), 0)[1], 0)

    groups = [(0, 1)] + [(2 * s - 1, 2 * s + 1) for s in range(1, hz)] + [(nz - 1, nz)]
    state = {"base": 0, "w": 0}
    here_k, here_m = {0}, {0}
    pending = {(k, m) for k in range(nz) for m in range(ny)}
    w_waits = [
        [(way, 1, w_order[way][n]) for way in range(2) if w_takes(way, 1, w_order[way][n])]
        for n in range(adapters)
    ]
    if hy > 1:
        half = adapters // 2
        w_waits += [[(way, 2, w_order[way][n]) for way in range(2)] for n in range(half)]
    w_waits = [pair for pair in w_waits if pair]

    def some_units(budget):
        while budget > 0:
            ready = sorted((m, k) for k, m in pending if k in here_k and m in here_m)
            if not ready:
                return
            m, low = ready[0]
            high = low
            while (m, high) in ready and high - low < budget:
                pending.discard((high, m))
                high += 1
            units(low, high, m, m + 1)
            budget -= high - low

    def next_w():
        if state["w"] == len(w_waits):
            return
        for way, step, j in w_waits[state["w"]]:
            w_copy(way, step, j).wait_recv()
            if step < hy and w_takes(way, step + 1, j):
                w_copy(way, step + 1, j).start()
        state["w"] += 1
        if state["w"] == len(w_waits):
            here_m.update(range(ny))
        elif hy > 1 and state["w"] == adapters:
            here_m.update((1, 2))

    def some_base(count):
        low = state["base"]
        high = min(nt, low + count)
        if low < high:
            lax.fori_loop(low, high, base_part, 0)
        state["base"] = high
        return high - low

    for step in range(1, hz):
        for c in range(CHUNKS):
            for way in range(2):
                z_copy(way, step, c).wait_recv()
                if z_takes(way, step + 1, c):
                    z_copy(way, step + 1, c).start()
            if c % 2 == 1:
                next_w()
            if c == CHUNKS - 1:
                for way in range(2):
                    k = slot_of(-step if way == 0 else step, nz)
                    wide_column(k, idz[k])
                    here_k.add(k)
            if c == 0:
                for way in range(2):
                    i_copy(way, step).wait_recv()
                    if once(way, step + 1, hz):
                        i_copy(way, step + 1).start()
                    if step < hy:
                        j_copy(way, step).wait_recv()
                        if once(way, step + 1, hy):
                            j_copy(way, step + 1).start()
            if not some_base(3):
                some_units(4)
    while state["w"] < len(w_waits):
        next_w()
    some_base(nt)

    def p_copy(g):
        span = pl.ds(groups[g][0], groups[g][1] - groups[g][0])
        return remote(
            acc.at[span, 1 - core], halves.at[span], p_send.at[g], p_recv.at[g], r, t + 1 - 2 * core
        )

    def a_copy(i, g):
        to = (x + i) % nx
        span = pl.ds(groups[g][0], groups[g][1] - groups[g][0])
        return remote(
            part.at[span, to], rs.at[i, span], a_send.at[g, i], a_recv.at[g, i], r, 2 * to + core
        )

    def pass_on(g):
        low, high = groups[g]
        p_copy(g).wait_recv()
        part[low:high] = acc[low:high, core] + halves[low:high]
        lax.fori_loop(1, nx, lambda i, _: (a_copy(i, g).start(), 0)[1], 0)

    def finish_a(g):
        low, high = groups[g]
        lax.fori_loop(1, nx, lambda i, _: (a_copy(i, g).wait_recv(), 0)[1], 0)
        total = part[low:high, x]
        for i in range(1, nx):
            total = total + rs[i, low:high]
        sh[low:high] = total.astype(BF16)

    def b_copy(k):
        d = 0 if k == 0 else next(d for d in range(1, nz) if slot_of(d, nz) == k)
        return remote(
            sh.at[k], hm.at[slot_of(-d, nz)], b_send.at[k], b_recv.at[slot_of(-d, nz)], at_z(d), t
        )

    def finish(g):
        low, high = groups[g]
        finish_a(g)
        for k in range(low, high):
            if k == 0:
                hm[0] = sh[0]
            else:
                b_copy(k).start()

    def rest_of(g):
        low, high = groups[g]
        for k in range(low, high):
            ms = [m for m in range(ny) if (k, m) in pending]
            mates = [n for n in range(k, high) if [m for m in range(ny) if (n, m) in pending] == ms]
            if ms and mates == list(range(k, k + len(mates))) and ms == list(range(ms[0], ny)):
                units(k, k + len(mates), ms[0], ny)
                pending.difference_update((n, m) for n in mates for m in ms)
            else:
                for m in ms:
                    units(k, k + 1, m, m + 1)
                    pending.discard((k, m))
        p_copy(g).start()

    def select_up(wanted, into, low, high):
        def one(k, _):
            first = (((z + shift_of(k, nz)) % nz) * ny + y) * adapters
            total = jnp.zeros((rank, 128), F32)
            for j in range(adapters):
                uses = jnp.where(wanted == first + j, 1.0, 0.0)
                uses = jnp.max(uses, axis=1, keepdims=True)
                total = total + uses * upz[k, j * rank : (j + 1) * rank].astype(F32)
            into[k] = total.astype(BF16)
            return 0

        lax.fori_loop(low, high, one, 0)

    u_groups = groups

    def s_copy(d, g):
        span = pl.ds(u_groups[g][0], u_groups[g][1] - u_groups[g][0])
        return remote(
            upsend.at[d, span], upsel.at[(-d) % ny, span], s_send.at[d, g], s_recv.at[d, g], at_y(d), t
        )

    rank_half = (lax.broadcasted_iota(jnp.int32, (rank, 128), 0) < rank // 2).astype(F32)

    def spread_up(e, g):
        def one(k, _):
            block = upsel[e, k].astype(F32)
            at = pl.ds(pl.multiple_of(k * rank, rank), rank)
            bd[e, at, 0:128] = (block * rank_half).astype(BF16)
            bd[e, at, 128:256] = (block * (1.0 - rank_half)).astype(BF16)
            return 0

        lax.fori_loop(u_groups[g][0], u_groups[g][1], one, 0)

    def u_pass(step):
        for h in range(2):
            for way in range(2):
                if u_takes(way, step, h):
                    u_copy(way, step, h).wait_recv()
                    if u_takes(way, step + 1, h):
                        u_copy(way, step + 1, h).start()

    def u_group(g):
        for d in range(1, ny):
            select_up(idy[d], upsend.at[d], *u_groups[g])
            s_copy(d, g).start()
        select_up(idx[...], upsel.at[0], *u_groups[g])
        spread_up(0, g)

    def s_finish(g):
        for d in range(1, ny):
            s_copy(d, g).wait_recv()
            spread_up(ny - d, g)

    for step in range(hz, hy):
        for way in range(2):
            j_copy(way, step).wait_recv()
            if once(way, step + 1, hy):
                j_copy(way, step + 1).start()
    j_copy(0, hy).wait_recv()
    own_u.wait()
    u_group(0)
    last = len(groups) - 1
    for g in range(last):
        rest_of(g)
        if g:
            pass_on(g - 1)
    for c in range(CHUNKS // 2):
        z_copy(0, hz, c).wait_recv()
        z_copy(1, hz, c + CHUNKS // 2).wait_recv()
        if c == 0:
            u_pass(1)
            pass_on(last - 1)
            u_group(1)
    i_copy(0, hz).wait_recv()
    wide_column(nz - 1, idz[nz - 1])
    rest_of(last)
    for g in range(last):
        finish(g)
    pass_on(last)
    if hz > 1:
        u_pass(2)
    finish(last)
    for step in range(2, hz):
        u_group(step)
        u_pass(step + 1)
    if hz > 1:
        u_group(hz)

    for k in range(1, nz):
        b_copy(k).wait_recv()
    mine = hm[0].astype(F32)
    for k in range(1, nz):
        mine = mine + hm[k].astype(F32)
    sr[share] = mine.astype(BF16)

    def c_copy(i):
        return remote(sr.at[share], sr.at[share], c_send.at[i], c_recv.at[i], r, (t + i) % nt)

    def c_arrival(i):
        src = (t + nt - i) % nt
        at = (src % 2) * nx + src // 2
        return remote(sr.at[at], sr.at[at], c_send.at[i], c_recv.at[i], r, src)

    lax.fori_loop(1, nt, lambda i, _: (c_copy(i).start(), 0)[1], 0)
    for g in range(hz + 1):
        s_finish(g)
    lax.fori_loop(1, nt, lambda i, _: (c_arrival(i).wait_recv(), 0)[1], 0)

    shrink = sr[...].astype(F32).reshape(rows, rank)
    wanted = colbuf[0]

    def delta_part(e, _):
        parts = []
        for k in range(nz):
            d = shift_of(k, nz)
            first = (((z + d) % nz) * ny + (y + e) % ny) * adapters
            uses = (wanted >= first) & (wanted < first + adapters)
            parts.append(jnp.where(uses, shrink, 0.0).astype(BF16))
        spread = jnp.concatenate(parts, axis=1)
        base[...] += SCALE * jnp.dot(spread, bd[e], preferred_element_type=F32)
        return 0

    lax.fori_loop(0, ny, delta_part, 0)
    projected = base[...].astype(BF16)
    stacked = jnp.concatenate([projected[:, 0:128], projected[:, 128:256]], axis=0)
    cache = jnp.dot(perm[...], stacked, preferred_element_type=F32).astype(BF16)
    kvs[...] = cache.reshape(replicas, cap2, 128)

    def o_copy(i):
        to = (r + i) % replicas
        return remote(
            kvs.at[to], out.at[pl.ds(pl.multiple_of(r * cap2, cap2), cap2)],
            o_send.at[i], o_recv.at[i], to, t,
        )

    def o_arrival(i):
        src = (r + replicas - i) % replicas
        return remote(
            kvs.at[src], out.at[pl.ds(pl.multiple_of(src * cap2, cap2), cap2)],
            o_send.at[i], o_recv.at[i], src, t,
        )

    lax.fori_loop(1, replicas, lambda i, _: (o_copy(i).start(), 0)[1], 0)
    own_o = pltpu.make_async_copy(
        kvs.at[r], out.at[pl.ds(pl.multiple_of(r * cap2, cap2), cap2)], local_sem.at[4 + nt]
    )
    own_o.start()

    for way in range(2):
        for step in range(1, hz + 1):
            for c in range(CHUNKS):
                if z_takes(way, step, c):
                    z_copy(way, step, c).wait_send()
            if once(way, step, hz):
                i_copy(way, step).wait_send()
            for h in range(2):
                if u_takes(way, step, h):
                    u_copy(way, step, h).wait_send()
        for step in range(1, hy + 1):
            for j in range(adapters):
                if w_takes(way, step, j):
                    w_copy(way, step, j).wait_send()
            if once(way, step, hy):
                j_copy(way, step).wait_send()
    for d in range(1, ny):
        for g in range(hz + 1):
            s_copy(d, g).wait_send()
    for k in range(1, nz):
        b_copy(k).wait_send()

    def tensor_sends(i, _):
        c_copy(i).wait_send()
        return 0

    lax.fori_loop(1, nt, tensor_sends, 0)
    for g in range(len(groups)):
        p_copy(g).wait_send()
        lax.fori_loop(1, nx, lambda i, _, g=g: (a_copy(i, g).wait_send(), 0)[1], 0)

    def cache_rows(i, _):
        o_copy(i).wait_send()
        o_arrival(i).wait_recv()
        return 0

    lax.fori_loop(1, replicas, cache_rows, 0)
    own_o.wait()


def shards(nz, hidden, key_value_weight, adapter_down_weight, adapter_up_weight, token_adapter_index, destinations):
    replicas = lax.axis_size("replica")
    nt = lax.axis_size("tensor")
    ny = replicas // nz
    rows, model = hidden.shape
    width = model // nt
    adapters, _, rank = adapter_down_weight.shape
    cols = key_value_weight.shape[2]
    cap2 = 2 * (2 * rows // replicas)
    sub = rows // nt
    hz, hy = nz // 2, ny // 2
    vm = pltpu.VMEM
    dma = pltpu.SemaphoreType.DMA
    scratch = [
        vm((nt, rows, width), BF16),
        vm((2 * model, cols), BF16),
        vm((2 * width, cols), F32),
        vm((rows, 2 * cols), F32),
        vm((nz, rows, width), BF16),
        vm((ny, adapters, width, rank), BF16),
        vm((nz, adapters * rank, cols), BF16),
        vm((nz, rows, rank), jnp.int32),
        vm((nz, 1, rows), jnp.int32),
        vm((ny, 1, rows), jnp.int32),
        vm((nz, 2, nt // 2, sub, rank), F32),
        vm((nz, nt // 2, sub, rank), F32),
        vm((nz, nt // 2, sub, rank), F32),
        vm((nt // 2, nz, sub, rank), F32),
        vm((nz, sub, rank), BF16),
        vm((nz, sub, rank), BF16),
        vm((nt, sub, rank), BF16),
        vm((ny, nz, rank, cols), BF16),
        vm((ny, nz, rank, cols), BF16),
        vm((ny, nz * rank, 2 * cols), BF16),
        vm((replicas * cap2, 2 * rows), BF16),
        vm((replicas, cap2, cols), BF16),
        dma((5 + nt,)),
        dma((2, hz + 1, CHUNKS)), dma((2, hz + 1, CHUNKS)),
        dma((2, hy + 1, adapters)), dma((2, hy + 1, adapters)),
        dma((2, hz + 1, 2)), dma((2, hz + 1, 2)),
        dma((2, hz + 1)), dma((2, hz + 1)),
        dma((2, hy + 1)), dma((2, hy + 1)),
        dma((hz + 1,)), dma((hz + 1,)),
        dma((hz + 1, nt)), dma((hz + 1, nt)),
        dma((nz,)), dma((nz,)),
        dma((nt,)), dma((nt,)),
        dma((ny, hz + 1)), dma((ny, hz + 1)),
        dma((replicas,)), dma((replicas,)),
    ]
    hbm = pl.BlockSpec(memory_space=pltpu.HBM)
    in_vmem = pl.BlockSpec(memory_space=pltpu.VMEM)
    cache = pl.pallas_call(
        functools.partial(kernel, (nz, ny, nt)),
        out_shape=jax.ShapeDtypeStruct((replicas * cap2, cols), BF16),
        in_specs=[hbm, hbm, hbm, hbm, in_vmem, in_vmem],
        out_specs=hbm,
        scratch_shapes=scratch,
        compiler_params=pltpu.CompilerParams(
            collective_id=0, has_side_effects=True, vmem_limit_bytes=56 * 1024 * 1024
        ),
        cost_estimate=pl.CostEstimate(
            flops=2 * rows * model * 2 * cols + 2 * nz * rows * width * ny * adapters * rank,
            bytes_accessed=2 * (rows * model + 2 * model * cols + adapters * width * rank),
            transcendentals=0,
        ),
    )(
        hidden,
        key_value_weight.reshape(2 * model, cols),
        adapter_down_weight,
        adapter_up_weight.reshape(adapters * rank, cols),
        token_adapter_index.reshape(1, rows),
        destinations.reshape(1, rows),
    )
    return cache.reshape(replicas * cap2 // 2, 2, cols)


def solution(mesh):
    placed = (
        P("replica", None),
        P(None, None, "tensor"),
        P("replica", "tensor", None),
        P("replica", None, None, "tensor"),
        P("replica"),
        P("replica", None),
    )
    return jax.shard_map(
        functools.partial(shards, RINGS), mesh=mesh, in_specs=placed,
        out_specs=P("replica", None, "tensor"), check_vma=False,
    )
```

```python
import functools

import jax
import jax.numpy as jnp
from jax import lax
from jax.experimental import pallas as pl
from jax.experimental.pallas import tpu as pltpu
from jax.sharding import PartitionSpec as P

RINGS = 8
USE = 8
SCALE = 0.5
CHUNKS = 4

BF16 = jnp.bfloat16
F32 = jnp.float32
MESH = pl.DeviceIdType.MESH


def slot_of(d, n):
    d %= n
    return 0 if d == 0 else (2 * d - 1 if d <= n // 2 else 2 * (n - d))


def shift_of(k, n):
    odd = k % 2
    return odd * ((k + 1) // 2) + (1 - odd) * ((n - k // 2) % n)


def kernel(
    dims,
    hid, kvw, down, up, idx, dest,
    out,
    hf, kvb, kvf, base, hbuf, wbuf, upz, colbuf, idz, idy, acc, halves, part, rs, lasts, sh, hm, sr, uses, upsend, upsel, bd, perm, kvs,
    local_sem, z_send, z_recv, w_send, w_recv, u_send, u_recv, i_send, i_recv, j_send, j_recv,
    l_send, l_recv, p_send, p_recv, a_send, a_recv, b_send, b_recv, c_send, c_recv, s_send, s_recv, o_send, o_recv,
):
    nz, ny, nt = dims
    rows, width = hbuf.shape[1], hbuf.shape[2]
    adapters, rank = wbuf.shape[1], wbuf.shape[3]
    sub = rows // nt
    piece = rows // CHUNKS
    cap2 = kvs.shape[1]
    replicas = nz * ny
    hz, hy = nz // 2, ny // 2

    r = lax.axis_index("replica")
    t = lax.axis_index("tensor")
    z, y = r // ny, r % ny
    nx = nt // 2
    x, core = t // 2, t % 2
    share = core * nx + x

    def at_z(d):
        return ((z + d + nz) % nz) * ny + y

    def at_y(d):
        return z * ny + (y + d + ny) % ny

    def remote(src, dst, send, recv, replica, tensor):
        return pltpu.make_async_remote_copy(
            src_ref=src, dst_ref=dst, send_sem=send, recv_sem=recv,
            device_id=(replica, tensor), device_id_type=MESH,
        )

    own_cols = pl.ds(pl.multiple_of(t * width, 128), width)
    own_h = pltpu.make_async_copy(hid.at[:, own_cols], hbuf.at[0], local_sem.at[0])
    own_w = pltpu.make_async_copy(down, wbuf.at[0], local_sem.at[1])
    own_u = pltpu.make_async_copy(up, upz.at[0], local_sem.at[2])
    own_k = pltpu.make_async_copy(kvw, kvb, local_sem.at[3])

    def full_copy(c):
        return pltpu.make_async_copy(
            hid.at[:, pl.ds(pl.multiple_of(c * width, 128), width)], hf.at[c], local_sem.at[4 + c]
        )

    own_h.start()
    own_w.start()
    own_u.start()
    own_k.start()
    lax.fori_loop(0, nt, lambda c, _: (full_copy(c).start(), 0)[1], 0)

    barrier = pltpu.get_barrier_semaphore()

    def greet_tensor(i, _):
        pl.semaphore_signal(barrier, inc=1, device_id=(r, (t + i) % nt), device_id_type=MESH)
        return 0

    for to in (at_z(1), at_z(-1), at_y(1), at_y(-1)):
        pl.semaphore_signal(barrier, inc=1, device_id=(to, t), device_id_type=MESH)
    lax.fori_loop(1, nt, greet_tensor, 0)
    pl.semaphore_wait(barrier, 4 + nt - 1)

    def z_copy(way, step, c):
        part = pl.ds(c * piece, piece)
        sign = -1 if way == 0 else 1
        to = at_z(1 if way == 0 else -1)
        dst = hbuf.at[slot_of(sign * step, nz), part]
        if step == 1:
            src = hid.at[part, own_cols]
        else:
            src = hbuf.at[slot_of(sign * (step - 1), nz), part]
        return remote(src, dst, z_send.at[way, step, c], z_recv.at[way, step, c], to, t)

    def z_takes(way, step, c):
        return step < hz or (step == hz and (c < CHUNKS // 2) == (way == 0))

    def u_copy(way, step, h):
        sign = -1 if way == 0 else 1
        to = at_z(1 if way == 0 else -1)
        n = upz.shape[1] // 2
        part = pl.ds(h * n, n)
        dst = upz.at[slot_of(sign * step, nz), part]
        if step == 1:
            src = up.at[part]
        else:
            src = upz.at[slot_of(sign * (step - 1), nz), part]
        return remote(src, dst, u_send.at[way, step, h], u_recv.at[way, step, h], to, t)

    def u_takes(way, step, h):
        return step < hz or (step == hz and h == way)

    def u_start():
        for h in range(2):
            for way in range(2):
                if u_takes(way, 1, h):
                    u_copy(way, 1, h).start()

    def w_copy(way, step, j):
        sign = -1 if way == 0 else 1
        to = at_y(1 if way == 0 else -1)
        dst = wbuf.at[slot_of(sign * step, ny), j]
        src = down.at[j] if step == 1 else wbuf.at[slot_of(sign * (step - 1), ny), j]
        return remote(src, dst, w_send.at[way, step, j], w_recv.at[way, step, j], to, t)

    def w_takes(way, step, j):
        return step < hy or (step == hy and (j < adapters // 2) == (way == 0))

    def i_copy(way, step):
        sign = -1 if way == 0 else 1
        src = idx if step == 1 else idz.at[slot_of(sign * (step - 1), nz)]
        dst = idz.at[slot_of(sign * step, nz)]
        to = at_z(1 if way == 0 else -1)
        return remote(src, dst, i_send.at[way, step], i_recv.at[way, step], to, t)

    def j_copy(way, step):
        sign = -1 if way == 0 else 1
        src = idx if step == 1 else idy.at[(sign * (step - 1)) % ny]
        dst = idy.at[(sign * step) % ny]
        to = at_y(1 if way == 0 else -1)
        return remote(src, dst, j_send.at[way, step], j_recv.at[way, step], to, t)

    def once(way, step, half_way):
        return step < half_way or (step == half_way and way == 0)

    for way in range(2):
        if once(way, 1, hz):
            i_copy(way, 1).start()
        if once(way, 1, hy):
            j_copy(way, 1).start()
    w_order = [list(range(adapters)), list(range(adapters // 2, adapters)) + list(range(adapters // 2))]
    for c in range(CHUNKS):
        for way in range(2):
            if z_takes(way, 1, c):
                z_copy(way, 1, c).start()
        for way in range(2):
            if c < adapters and w_takes(way, 1, w_order[way][c]):
                w_copy(way, 1, w_order[way][c]).start()
    u_start()

    eye = lax.broadcasted_iota(jnp.int32, (rows, rows), 0) == lax.broadcasted_iota(
        jnp.int32, (rows, rows), 1
    )

    def column(row):
        wide = jnp.broadcast_to(row, (rows, rows))
        return jnp.sum(jnp.where(eye, wide, 0.0), axis=1, keepdims=True)

    def base_part(c, _):
        words = 2 * width
        at = pl.ds(pl.multiple_of(c * words, 128), words)
        kvf[...] = kvb[at, :].astype(F32)
        keys = kvf[pl.ds(0, width, stride=2), :].astype(BF16)
        values = kvf[pl.ds(1, width, stride=2), :].astype(BF16)
        both = jnp.concatenate([keys, values], axis=1)
        base[...] += jnp.dot(hf[c], both, preferred_element_type=F32)
        return 0

    def unit(k, m):
        mate = shift_of(m, ny)
        first = (z * ny + (y + mate) % ny) * adapters
        wanted = colbuf[k]
        total = acc[k].reshape(rows, rank)
        h = hbuf[k]
        for pair in range(adapters // 2):
            w = jnp.concatenate([wbuf[m, 2 * pair], wbuf[m, 2 * pair + 1]], axis=1)
            got = jnp.dot(h, w, preferred_element_type=F32)
            for j in range(2):
                mine = wanted == first + 2 * pair + j
                total = total + jnp.where(mine, got[:, j * rank : (j + 1) * rank], 0.0)
        acc[k] = total.reshape(2, nx, sub, rank)

    def units(k_low, k_high, m_low, m_high):
        count = m_high - m_low

        def one(i, _):
            unit(k_low + i // count, m_low + i % count)
            return 0

        if (k_high - k_low) * count == 1:
            unit(k_low, m_low)
        else:
            lax.fori_loop(0, (k_high - k_low) * count, one, 0)

    base[...] = jnp.zeros_like(base)
    acc[...] = jnp.zeros_like(acc)
    to_row = dest[...].astype(F32)
    to_col = column(to_row)
    before = lax.broadcasted_iota(jnp.int32, (rows, rows), 0) < lax.broadcasted_iota(
        jnp.int32, (rows, rows), 1
    )
    earlier = jnp.where(before & (to_col == to_row), 1.0, 0.0)
    order = jnp.sum(earlier, axis=0, keepdims=True)
    place = to_row * float(cap2) + order * 2.0
    n_perm = perm.shape[0]
    for p in range(2):
        target = lax.broadcasted_iota(jnp.int32, (n_perm, rows), 0).astype(F32)
        perm[:, p * rows : (p + 1) * rows] = jnp.where(target == place + float(p), 1.0, 0.0).astype(
            BF16
        )

    def wide_column(k, row):
        colbuf[k] = jnp.broadcast_to(column(row.astype(F32)), (rows, rank)).astype(jnp.int32)

    wide_column(0, idx[...])
    own_h.wait()
    own_w.wait()
    own_k.wait()
    lax.fori_loop(0, nt, lambda c, _: (full_copy(c).wait(), 0)[1], 0)

    last = hz
    groups = [(0, 1)] + [(2 * s - 1, 2 * s + 1) for s in range(1, hz)] + [(nz - 1, nz)]
    state = {"base": 0, "w": 0, "up": 0}
    here_k, here_m = {0}, {0}
    pending = {(k, m) for k in range(nz) for m in range(ny)}
    w_waits = [
        [(way, 1, w_order[way][n]) for way in range(2) if w_takes(way, 1, w_order[way][n])]
        for n in range(adapters)
    ]
    if hy > 1:
        half = adapters // 2
        w_waits += [[(way, 2, w_order[way][n]) for way in range(2)] for n in range(half)]
    w_waits = [pair for pair in w_waits if pair]

    def mark_uses(e, wanted):
        count = nz * adapters
        row = lax.broadcasted_iota(jnp.int32, (count, rows), 0)
        number = jnp.zeros((count, rows), jnp.int32)
        for k in range(nz):
            first = (((z + shift_of(k, nz)) % nz) * ny + y) * adapters
            here = (row >= k * adapters) & (row < (k + 1) * adapters)
            number = jnp.where(here, first + row - k * adapters, number)
        found = jnp.where(number == jnp.broadcast_to(wanted, (count, rows)), 1.0, 0.0)
        uses[e] = jnp.broadcast_to(jnp.max(found, axis=1, keepdims=True), (count, 128))

    def select_up(e, into, low, high):
        for k in range(low, high):
            total = jnp.zeros((rank, 128), F32)
            for j in range(adapters):
                at = k * adapters + j
                total = total + uses[e, at : at + 1] * upz[k, j * rank : (j + 1) * rank].astype(F32)
            into[k] = total.astype(BF16)

    u_groups = groups

    def s_copy(d, g):
        span = pl.ds(u_groups[g][0], u_groups[g][1] - u_groups[g][0])
        return remote(
            upsend.at[d, span], upsel.at[(-d) % ny, span], s_send.at[d, g], s_recv.at[d, g], at_y(d), t
        )

    rank_half = (lax.broadcasted_iota(jnp.int32, (rank, 128), 0) < rank // 2).astype(F32)

    def spread_up(e, g):
        def one(k, _):
            block = upsel[e, k].astype(F32)
            at = pl.ds(pl.multiple_of(k * rank, rank), rank)
            bd[e, at, 0:128] = (block * rank_half).astype(BF16)
            bd[e, at, 128:256] = (block * (1.0 - rank_half)).astype(BF16)
            return 0

        lax.fori_loop(u_groups[g][0], u_groups[g][1], one, 0)

    def u_group(g):
        for d in range(1, ny):
            select_up(d, upsend.at[d], *u_groups[g])
            s_copy(d, g).start()
        select_up(0, upsel.at[0], *u_groups[g])
        spread_up(0, g)

    def early_up():
        if state["up"]:
            return
        state["up"] = 1
        j_copy(0, hy).wait_recv()
        own_u.wait()
        mark_uses(0, idx[...])
        for d in range(1, ny):
            mark_uses(d, idy[d])
        u_group(0)

    def some_units(budget):
        while budget > 0:
            ready = sorted((m, k) for k, m in pending if k in here_k and m in here_m)
            if not ready:
                return
            m, low = ready[0]
            high = low
            while (m, high) in ready and high - low < budget:
                pending.discard((high, m))
                high += 1
            units(low, high, m, m + 1)
            budget -= high - low

    def next_w():
        if state["w"] == len(w_waits):
            return
        for way, step, j in w_waits[state["w"]]:
            w_copy(way, step, j).wait_recv()
            if step < hy and w_takes(way, step + 1, j):
                w_copy(way, step + 1, j).start()
        state["w"] += 1
        if state["w"] == len(w_waits):
            here_m.update(range(ny))
        elif hy > 1 and state["w"] == adapters:
            here_m.update((1, 2))

    def some_base(count):
        low = state["base"]
        high = min(nt, low + count)
        if low < high:
            lax.fori_loop(low, high, base_part, 0)
        state["base"] = high
        return high - low

    for step in range(1, hz):
        for c in range(CHUNKS):
            for way in range(2):
                z_copy(way, step, c).wait_recv()
                if z_takes(way, step + 1, c):
                    z_copy(way, step + 1, c).start()
            if c % 2 == 1:
                next_w()
            if c == CHUNKS - 1:
                for way in range(2):
                    k = slot_of(-step if way == 0 else step, nz)
                    wide_column(k, idz[k])
                    here_k.add(k)
            if c == 0:
                for way in range(2):
                    i_copy(way, step).wait_recv()
                    if once(way, step + 1, hz):
                        i_copy(way, step + 1).start()
                    if step < hy:
                        j_copy(way, step).wait_recv()
                        if once(way, step + 1, hy):
                            j_copy(way, step + 1).start()
            if not some_base(3):
                some_units(4)
            if step == hy and c == 2:
                early_up()
    while state["w"] < len(w_waits):
        next_w()
    some_base(nt)

    def p_copy(g):
        span = pl.ds(groups[g][0], groups[g][1] - groups[g][0])
        return remote(
            acc.at[span, 1 - core], halves.at[span], p_send.at[g], p_recv.at[g], r, t + 1 - 2 * core
        )

    def a_copy(i, g):
        to = (x + i) % nx
        span = pl.ds(groups[g][0], groups[g][1] - groups[g][0])
        return remote(
            part.at[span, to], rs.at[i, span], a_send.at[g, i], a_recv.at[g, i], r, 2 * to + core
        )

    def pass_on(g):
        low, high = groups[g]
        p_copy(g).wait_recv()
        part[low:high] = acc[low:high, core] + halves[low:high]
        lax.fori_loop(1, nx, lambda i, _: (a_copy(i, g).start(), 0)[1], 0)

    def l_copy(i):
        to = (t + i) % nt
        return remote(acc.at[nz - 1, to % 2, to // 2], lasts.at[i], l_send.at[i], l_recv.at[i], r, to)

    def finish_a(g):
        low, high = groups[g]
        if g == last:
            lax.fori_loop(1, nt, lambda i, _: (l_copy(i).wait_recv(), 0)[1], 0)
            total = acc[nz - 1, core, x]
            for i in range(1, nt):
                total = total + lasts[i]
            sh[nz - 1] = total.astype(BF16)
            return
        lax.fori_loop(1, nx, lambda i, _: (a_copy(i, g).wait_recv(), 0)[1], 0)
        total = part[low:high, x]
        for i in range(1, nx):
            total = total + rs[i, low:high]
        sh[low:high] = total.astype(BF16)

    def b_copy(k):
        d = 0 if k == 0 else next(d for d in range(1, nz) if slot_of(d, nz) == k)
        return remote(
            sh.at[k], hm.at[slot_of(-d, nz)], b_send.at[k], b_recv.at[slot_of(-d, nz)], at_z(d), t
        )

    def finish(g):
        low, high = groups[g]
        finish_a(g)
        for k in range(low, high):
            if k == 0:
                hm[0] = sh[0]
            else:
                b_copy(k).start()

    def rest_of(g):
        low, high = groups[g]
        for k in range(low, high):
            ms = [m for m in range(ny) if (k, m) in pending]
            mates = [n for n in range(k, high) if [m for m in range(ny) if (n, m) in pending] == ms]
            if ms and mates == list(range(k, k + len(mates))) and ms == list(range(ms[0], ny)):
                units(k, k + len(mates), ms[0], ny)
                pending.difference_update((n, m) for n in mates for m in ms)
            else:
                for m in ms:
                    units(k, k + 1, m, m + 1)
                    pending.discard((k, m))
        if g < last:
            p_copy(g).start()
        else:
            lax.fori_loop(1, nt, lambda i, _: (l_copy(i).start(), 0)[1], 0)

    def u_pass(step):
        for h in range(2):
            for way in range(2):
                if u_takes(way, step, h):
                    u_copy(way, step, h).wait_recv()
                    if u_takes(way, step + 1, h):
                        u_copy(way, step + 1, h).start()

    def s_finish(g):
        for d in range(1, ny):
            s_copy(d, g).wait_recv()
            spread_up(ny - d, g)

    for step in range(hz, hy):
        for way in range(2):
            j_copy(way, step).wait_recv()
            if once(way, step + 1, hy):
                j_copy(way, step + 1).start()
    early_up()
    for g in range(last):
        rest_of(g)
        if g:
            pass_on(g - 1)
    for c in range(CHUNKS // 2):
        z_copy(0, hz, c).wait_recv()
        z_copy(1, hz, c + CHUNKS // 2).wait_recv()
        if c == 0:
            u_pass(1)
            pass_on(last - 1)
    i_copy(0, hz).wait_recv()
    wide_column(nz - 1, idz[nz - 1])
    rest_of(last)
    for g in range(last):
        finish(g)
    u_group(1)
    if hz > 1:
        u_pass(2)
    finish(last)
    if hz > 1:
        u_group(2)
    for step in range(3, hz):
        u_pass(step)
        u_group(step)

    for k in range(1, nz):
        b_copy(k).wait_recv()
    mine = hm[0].astype(F32)
    for k in range(1, nz):
        mine = mine + hm[k].astype(F32)
    sr[share] = mine.astype(BF16)

    def c_copy(i):
        return remote(sr.at[share], sr.at[share], c_send.at[i], c_recv.at[i], r, (t + i) % nt)

    def c_arrival(i):
        src = (t + nt - i) % nt
        at = (src % 2) * nx + src // 2
        return remote(sr.at[at], sr.at[at], c_send.at[i], c_recv.at[i], r, src)

    lax.fori_loop(1, nt, lambda i, _: (c_copy(i).start(), 0)[1], 0)
    if hz > 2:
        u_pass(hz)
        u_group(hz)
    for g in range(hz + 1):
        s_finish(g)
    lax.fori_loop(1, nt, lambda i, _: (c_arrival(i).wait_recv(), 0)[1], 0)

    shrink = sr[...].astype(F32).reshape(rows, rank)
    wanted = colbuf[0]

    def delta_part(e, _):
        parts = []
        for k in range(nz):
            d = shift_of(k, nz)
            first = (((z + d) % nz) * ny + (y + e) % ny) * adapters
            uses = (wanted >= first) & (wanted < first + adapters)
            parts.append(jnp.where(uses, shrink, 0.0).astype(BF16))
        spread = jnp.concatenate(parts, axis=1)
        base[...] += SCALE * jnp.dot(spread, bd[e], preferred_element_type=F32)
        return 0

    lax.fori_loop(0, ny, delta_part, 0)
    projected = base[...].astype(BF16)
    stacked = jnp.concatenate([projected[:, 0:128], projected[:, 128:256]], axis=0)
    cache = jnp.dot(perm[...], stacked, preferred_element_type=F32).astype(BF16)
    kvs[...] = cache.reshape(replicas, cap2, 128)

    def o_copy(i):
        to = ((z + shift_of(i // ny, nz)) % nz) * ny + (y + i % ny) % ny
        return remote(
            kvs.at[to], out.at[pl.ds(pl.multiple_of(r * cap2, cap2), cap2)],
            o_send.at[i], o_recv.at[i], to, t,
        )

    def o_arrival(i):
        src = ((z + nz - shift_of(i // ny, nz)) % nz) * ny + (y + ny - i % ny) % ny
        return remote(
            kvs.at[src], out.at[pl.ds(pl.multiple_of(src * cap2, cap2), cap2)],
            o_send.at[i], o_recv.at[i], src, t,
        )

    lax.fori_loop(1, replicas, lambda i, _: (o_copy(replicas - i).start(), 0)[1], 0)
    own_o = pltpu.make_async_copy(
        kvs.at[r], out.at[pl.ds(pl.multiple_of(r * cap2, cap2), cap2)], local_sem.at[4 + nt]
    )
    own_o.start()

    for way in range(2):
        for step in range(1, hz + 1):
            for c in range(CHUNKS):
                if z_takes(way, step, c):
                    z_copy(way, step, c).wait_send()
            if once(way, step, hz):
                i_copy(way, step).wait_send()
            for h in range(2):
                if u_takes(way, step, h):
                    u_copy(way, step, h).wait_send()
        for step in range(1, hy + 1):
            for j in range(adapters):
                if w_takes(way, step, j):
                    w_copy(way, step, j).wait_send()
            if once(way, step, hy):
                j_copy(way, step).wait_send()
    for d in range(1, ny):
        for g in range(hz + 1):
            s_copy(d, g).wait_send()
    for k in range(1, nz):
        b_copy(k).wait_send()

    def tensor_sends(i, _):
        c_copy(i).wait_send()
        l_copy(i).wait_send()
        return 0

    lax.fori_loop(1, nt, tensor_sends, 0)
    for g in range(last):
        p_copy(g).wait_send()
        lax.fori_loop(1, nx, lambda i, _, g=g: (a_copy(i, g).wait_send(), 0)[1], 0)

    def cache_rows(i, _):
        o_copy(i).wait_send()
        o_arrival(i).wait_recv()
        return 0

    lax.fori_loop(1, replicas, cache_rows, 0)
    own_o.wait()


def shards(nz, hidden, key_value_weight, adapter_down_weight, adapter_up_weight, token_adapter_index, destinations):
    replicas = lax.axis_size("replica")
    nt = lax.axis_size("tensor")
    ny = replicas // nz
    rows, model = hidden.shape
    width = model // nt
    adapters, _, rank = adapter_down_weight.shape
    cols = key_value_weight.shape[2]
    cap2 = 2 * (2 * rows // replicas)
    sub = rows // nt
    hz, hy = nz // 2, ny // 2
    vm = pltpu.VMEM
    dma = pltpu.SemaphoreType.DMA
    scratch = [
        vm((nt, rows, width), BF16),
        vm((2 * model, cols), BF16),
        vm((2 * width, cols), F32),
        vm((rows, 2 * cols), F32),
        vm((nz, rows, width), BF16),
        vm((ny, adapters, width, rank), BF16),
        vm((nz, adapters * rank, cols), BF16),
        vm((nz, rows, rank), jnp.int32),
        vm((nz, 1, rows), jnp.int32),
        vm((ny, 1, rows), jnp.int32),
        vm((nz, 2, nt // 2, sub, rank), F32),
        vm((nz, nt // 2, sub, rank), F32),
        vm((nz, nt // 2, sub, rank), F32),
        vm((nt // 2, nz, sub, rank), F32),
        vm((nt, sub, rank), F32),
        vm((nz, sub, rank), BF16),
        vm((nz, sub, rank), BF16),
        vm((nt, sub, rank), BF16),
        vm((ny, nz * adapters, 128), F32),
        vm((ny, nz, rank, cols), BF16),
        vm((ny, nz, rank, cols), BF16),
        vm((ny, nz * rank, 2 * cols), BF16),
        vm((replicas * cap2, 2 * rows), BF16),
        vm((replicas, cap2, cols), BF16),
        dma((5 + nt,)),
        dma((2, hz + 1, CHUNKS)), dma((2, hz + 1, CHUNKS)),
        dma((2, hy + 1, adapters)), dma((2, hy + 1, adapters)),
        dma((2, hz + 1, 2)), dma((2, hz + 1, 2)),
        dma((2, hz + 1)), dma((2, hz + 1)),
        dma((2, hy + 1)), dma((2, hy + 1)),
        dma((nt,)), dma((nt,)),
        dma((hz + 1,)), dma((hz + 1,)),
        dma((hz + 1, nt)), dma((hz + 1, nt)),
        dma((nz,)), dma((nz,)),
        dma((nt,)), dma((nt,)),
        dma((ny, hz + 1)), dma((ny, hz + 1)),
        dma((replicas,)), dma((replicas,)),
    ]
    hbm = pl.BlockSpec(memory_space=pltpu.HBM)
    in_vmem = pl.BlockSpec(memory_space=pltpu.VMEM)
    cache = pl.pallas_call(
        functools.partial(kernel, (nz, ny, nt)),
        out_shape=pltpu.VMEM((replicas * cap2, cols), BF16),
        in_specs=[hbm, hbm, hbm, hbm, in_vmem, in_vmem],
        out_specs=in_vmem,
        scratch_shapes=scratch,
        compiler_params=pltpu.CompilerParams(
            collective_id=0, has_side_effects=True, vmem_limit_bytes=56 * 1024 * 1024
        ),
        cost_estimate=pl.CostEstimate(
            flops=2 * rows * model * 2 * cols + 2 * nz * rows * width * ny * adapters * rank,
            bytes_accessed=2 * (rows * model + 2 * model * cols + adapters * width * rank),
            transcendentals=0,
        ),
    )(
        hidden,
        key_value_weight.reshape(2 * model, cols),
        adapter_down_weight,
        adapter_up_weight.reshape(adapters * rank, cols),
        token_adapter_index.reshape(1, rows),
        destinations.reshape(1, rows),
    )
    return cache.reshape(replicas * cap2 // 2, 2, cols)


def solution(mesh):
    placed = (
        P("replica", None),
        P(None, None, "tensor"),
        P("replica", "tensor", None),
        P("replica", None, None, "tensor"),
        P("replica"),
        P("replica", None),
    )
    return jax.shard_map(
        functools.partial(shards, RINGS), mesh=mesh, in_specs=placed,
        out_specs=P("replica", None, "tensor"), check_vma=False,
    )
```

```python
import functools

import jax
import jax.numpy as jnp
from jax import lax
from jax.experimental import pallas as pl
from jax.experimental.pallas import tpu as pltpu
from jax.sharding import PartitionSpec as P

RINGS = 8
USE = 8
SCALE = 0.5
CHUNKS = 4

BF16 = jnp.bfloat16
F32 = jnp.float32
MESH = pl.DeviceIdType.MESH


def slot_of(d, n):
    d %= n
    return 0 if d == 0 else (2 * d - 1 if d <= n // 2 else 2 * (n - d))


def shift_of(k, n):
    odd = k % 2
    return odd * ((k + 1) // 2) + (1 - odd) * ((n - k // 2) % n)


def kernel(
    dims,
    hid, kvw, down, up, idx, dest,
    out,
    hf, kvb, kvf, base, hbuf, wbuf, upz, colbuf, idz, idy, acc, halves, part, rs, lasts, sh, hm, sr, uses, upsend, upsel, bd, perm, kvs,
    local_sem, z_send, z_recv, w_send, w_recv, u_send, u_recv, i_send, i_recv, j_send, j_recv,
    l_send, l_recv, p_send, p_recv, a_send, a_recv, b_send, b_recv, c_send, c_recv, s_send, s_recv, o_send, o_recv,
):
    nz, ny, nt = dims
    rows, width = hbuf.shape[1], hbuf.shape[2]
    adapters, rank = wbuf.shape[1], wbuf.shape[3]
    sub = rows // nt
    piece = rows // CHUNKS
    cap2 = kvs.shape[1]
    replicas = nz * ny
    hz, hy = nz // 2, ny // 2

    r = lax.axis_index("replica")
    t = lax.axis_index("tensor")
    z, y = r // ny, r % ny
    nx = nt // 2
    x, core = t // 2, t % 2
    share = core * nx + x

    def at_z(d):
        return ((z + d + nz) % nz) * ny + y

    def at_y(d):
        return z * ny + (y + d + ny) % ny

    def remote(src, dst, send, recv, replica, tensor):
        return pltpu.make_async_remote_copy(
            src_ref=src, dst_ref=dst, send_sem=send, recv_sem=recv,
            device_id=(replica, tensor), device_id_type=MESH,
        )

    barrier = pltpu.get_barrier_semaphore()

    def greet_tensor(i, _):
        pl.semaphore_signal(barrier, inc=1, device_id=(r, (t + i) % nt), device_id_type=MESH)
        return 0

    for to in (at_z(1), at_z(-1), at_y(1), at_y(-1)):
        pl.semaphore_signal(barrier, inc=1, device_id=(to, t), device_id_type=MESH)
    lax.fori_loop(1, nt, greet_tensor, 0)

    own_cols = pl.ds(pl.multiple_of(t * width, 128), width)
    own_h = pltpu.make_async_copy(hid.at[:, own_cols], hbuf.at[0], local_sem.at[0])
    own_w = pltpu.make_async_copy(down, wbuf.at[0], local_sem.at[1])
    own_u = pltpu.make_async_copy(up, upz.at[0], local_sem.at[2])
    own_k = pltpu.make_async_copy(kvw, kvb, local_sem.at[3])

    def full_copy(c):
        return pltpu.make_async_copy(
            hid.at[:, pl.ds(pl.multiple_of(c * width, 128), width)], hf.at[c], local_sem.at[4 + c]
        )

    own_h.start()
    own_w.start()
    own_u.start()
    own_k.start()
    lax.fori_loop(0, nt, lambda c, _: (full_copy(c).start(), 0)[1], 0)

    pl.semaphore_wait(barrier, 4 + nt - 1)

    def z_copy(way, step, c):
        part = pl.ds(c * piece, piece)
        sign = -1 if way == 0 else 1
        to = at_z(1 if way == 0 else -1)
        dst = hbuf.at[slot_of(sign * step, nz), part]
        if step == 1:
            src = hid.at[part, own_cols]
        else:
            src = hbuf.at[slot_of(sign * (step - 1), nz), part]
        return remote(src, dst, z_send.at[way, step, c], z_recv.at[way, step, c], to, t)

    def z_takes(way, step, c):
        return step < hz or (step == hz and (c < CHUNKS // 2) == (way == 0))

    def u_copy(way, step, h):
        sign = -1 if way == 0 else 1
        to = at_z(1 if way == 0 else -1)
        n = upz.shape[1] // 2
        part = pl.ds(h * n, n)
        dst = upz.at[slot_of(sign * step, nz), part]
        if step == 1:
            src = up.at[part]
        else:
            src = upz.at[slot_of(sign * (step - 1), nz), part]
        return remote(src, dst, u_send.at[way, step, h], u_recv.at[way, step, h], to, t)

    def u_takes(way, step, h):
        return step < hz or (step == hz and h == way)

    def u_start():
        for h in range(2):
            for way in range(2):
                if u_takes(way, 1, h):
                    u_copy(way, 1, h).start()

    def w_copy(way, step, j):
        sign = -1 if way == 0 else 1
        to = at_y(1 if way == 0 else -1)
        dst = wbuf.at[slot_of(sign * step, ny), j]
        src = down.at[j] if step == 1 else wbuf.at[slot_of(sign * (step - 1), ny), j]
        return remote(src, dst, w_send.at[way, step, j], w_recv.at[way, step, j], to, t)

    def w_takes(way, step, j):
        return step < hy or (step == hy and (j < adapters // 2) == (way == 0))

    def i_copy(way, step):
        sign = -1 if way == 0 else 1
        src = idx if step == 1 else idz.at[slot_of(sign * (step - 1), nz)]
        dst = idz.at[slot_of(sign * step, nz)]
        to = at_z(1 if way == 0 else -1)
        return remote(src, dst, i_send.at[way, step], i_recv.at[way, step], to, t)

    def j_copy(way, step):
        sign = -1 if way == 0 else 1
        src = idx if step == 1 else idy.at[(sign * (step - 1)) % ny]
        dst = idy.at[(sign * step) % ny]
        to = at_y(1 if way == 0 else -1)
        return remote(src, dst, j_send.at[way, step], j_recv.at[way, step], to, t)

    def once(way, step, half_way):
        return step < half_way or (step == half_way and way == 0)

    for way in range(2):
        if once(way, 1, hz):
            i_copy(way, 1).start()
        if once(way, 1, hy):
            j_copy(way, 1).start()
    w_order = [list(range(adapters)), list(range(adapters // 2, adapters)) + list(range(adapters // 2))]
    for c in range(CHUNKS):
        for way in range(2):
            if z_takes(way, 1, c):
                z_copy(way, 1, c).start()
        for way in range(2):
            if c < adapters and w_takes(way, 1, w_order[way][c]):
                w_copy(way, 1, w_order[way][c]).start()
    u_start()

    eye = lax.broadcasted_iota(jnp.int32, (rows, rows), 0) == lax.broadcasted_iota(
        jnp.int32, (rows, rows), 1
    )

    def column(row):
        wide = jnp.broadcast_to(row, (rows, rows))
        return jnp.sum(jnp.where(eye, wide, 0.0), axis=1, keepdims=True)

    def base_part(c, _):
        words = 2 * width
        at = pl.ds(pl.multiple_of(c * words, 128), words)
        kvf[...] = kvb[at, :].astype(F32)
        keys = kvf[pl.ds(0, width, stride=2), :].astype(BF16)
        values = kvf[pl.ds(1, width, stride=2), :].astype(BF16)
        both = jnp.concatenate([keys, values], axis=1)
        base[...] += jnp.dot(hf[c], both, preferred_element_type=F32)
        return 0

    def unit(k, m):
        mate = shift_of(m, ny)
        first = (z * ny + (y + mate) % ny) * adapters
        wanted = colbuf[k]
        total = acc[k].reshape(rows, rank)
        h = hbuf[k]
        for pair in range(adapters // 2):
            w = jnp.concatenate([wbuf[m, 2 * pair], wbuf[m, 2 * pair + 1]], axis=1)
            got = jnp.dot(h, w, preferred_element_type=F32)
            for j in range(2):
                mine = wanted == first + 2 * pair + j
                total = total + jnp.where(mine, got[:, j * rank : (j + 1) * rank], 0.0)
        acc[k] = total.reshape(2, nx, sub, rank)

    def units(k_low, k_high, m_low, m_high):
        count = m_high - m_low

        def one(i, _):
            unit(k_low + i // count, m_low + i % count)
            return 0

        if (k_high - k_low) * count == 1:
            unit(k_low, m_low)
        else:
            lax.fori_loop(0, (k_high - k_low) * count, one, 0)

    base[...] = jnp.zeros_like(base)
    acc[...] = jnp.zeros_like(acc)
    to_row = dest[...].astype(F32)
    to_col = column(to_row)
    before = lax.broadcasted_iota(jnp.int32, (rows, rows), 0) < lax.broadcasted_iota(
        jnp.int32, (rows, rows), 1
    )
    earlier = jnp.where(before & (to_col == to_row), 1.0, 0.0)
    order = jnp.sum(earlier, axis=0, keepdims=True)
    place = to_row * float(cap2) + order * 2.0
    n_perm = perm.shape[0]
    for p in range(2):
        target = lax.broadcasted_iota(jnp.int32, (n_perm, rows), 0).astype(F32)
        perm[:, p * rows : (p + 1) * rows] = jnp.where(target == place + float(p), 1.0, 0.0).astype(
            BF16
        )

    def wide_column(k, row):
        colbuf[k] = jnp.broadcast_to(column(row.astype(F32)), (rows, rank)).astype(jnp.int32)

    wide_column(0, idx[...])
    own_h.wait()
    own_w.wait()
    own_k.wait()
    lax.fori_loop(0, nt, lambda c, _: (full_copy(c).wait(), 0)[1], 0)

    last = hz
    groups = [(0, 1)] + [(2 * s - 1, 2 * s + 1) for s in range(1, hz)] + [(nz - 1, nz)]
    state = {"base": 0, "w": 0, "up": 0}
    here_k, here_m = {0}, {0}
    pending = {(k, m) for k in range(nz) for m in range(ny)}
    w_waits = [
        [(way, 1, w_order[way][n]) for way in range(2) if w_takes(way, 1, w_order[way][n])]
        for n in range(adapters)
    ]
    if hy > 1:
        half = adapters // 2
        w_waits += [[(way, 2, w_order[way][n]) for way in range(2)] for n in range(half)]
    w_waits = [pair for pair in w_waits if pair]

    def mark_uses(e, wanted):
        count = nz * adapters
        row = lax.broadcasted_iota(jnp.int32, (count, rows), 0)
        number = jnp.zeros((count, rows), jnp.int32)
        for k in range(nz):
            first = (((z + shift_of(k, nz)) % nz) * ny + y) * adapters
            here = (row >= k * adapters) & (row < (k + 1) * adapters)
            number = jnp.where(here, first + row - k * adapters, number)
        found = jnp.where(number == jnp.broadcast_to(wanted, (count, rows)), 1.0, 0.0)
        uses[e] = jnp.broadcast_to(jnp.max(found, axis=1, keepdims=True), (count, 128))

    def select_up(e, into, low, high):
        for k in range(low, high):
            total = jnp.zeros((rank, 128), F32)
            for j in range(adapters):
                at = k * adapters + j
                total = total + uses[e, at : at + 1] * upz[k, j * rank : (j + 1) * rank].astype(F32)
            into[k] = total.astype(BF16)

    u_groups = groups

    def s_copy(d, g):
        span = pl.ds(u_groups[g][0], u_groups[g][1] - u_groups[g][0])
        return remote(
            upsend.at[d, span], upsel.at[(-d) % ny, span], s_send.at[d, g], s_recv.at[d, g], at_y(d), t
        )

    rank_half = (lax.broadcasted_iota(jnp.int32, (rank, 128), 0) < rank // 2).astype(F32)

    def spread_up(e, g):
        def one(k, _):
            block = upsel[e, k].astype(F32)
            at = pl.ds(pl.multiple_of(k * rank, rank), rank)
            bd[e, at, 0:128] = (block * rank_half).astype(BF16)
            bd[e, at, 128:256] = (block * (1.0 - rank_half)).astype(BF16)
            return 0

        lax.fori_loop(u_groups[g][0], u_groups[g][1], one, 0)

    def u_group(g):
        for d in range(1, ny):
            select_up(d, upsend.at[d], *u_groups[g])
            s_copy(d, g).start()
        select_up(0, upsel.at[0], *u_groups[g])
        spread_up(0, g)

    def early_up():
        if state["up"]:
            return
        state["up"] = 1
        j_copy(0, hy).wait_recv()
        own_u.wait()
        mark_uses(0, idx[...])
        for d in range(1, ny):
            mark_uses(d, idy[d])
        u_group(0)

    def some_units(budget):
        while budget > 0:
            ready = sorted((m, k) for k, m in pending if k in here_k and m in here_m)
            if not ready:
                return
            m, low = ready[0]
            high = low
            while (m, high) in ready and high - low < budget:
                pending.discard((high, m))
                high += 1
            units(low, high, m, m + 1)
            budget -= high - low

    def next_w():
        if state["w"] == len(w_waits):
            return
        for way, step, j in w_waits[state["w"]]:
            w_copy(way, step, j).wait_recv()
            if step < hy and w_takes(way, step + 1, j):
                w_copy(way, step + 1, j).start()
        state["w"] += 1
        if state["w"] == len(w_waits):
            here_m.update(range(ny))
        elif hy > 1 and state["w"] == adapters:
            here_m.update((1, 2))

    def some_base(count):
        low = state["base"]
        high = min(nt, low + count)
        if low < high:
            lax.fori_loop(low, high, base_part, 0)
        state["base"] = high
        return high - low

    for step in range(1, hz):
        for c in range(CHUNKS):
            for way in range(2):
                z_copy(way, step, c).wait_recv()
                if z_takes(way, step + 1, c):
                    z_copy(way, step + 1, c).start()
            if c % 2 == 1:
                next_w()
            if c == CHUNKS - 1:
                for way in range(2):
                    k = slot_of(-step if way == 0 else step, nz)
                    wide_column(k, idz[k])
                    here_k.add(k)
            if c == 0:
                for way in range(2):
                    i_copy(way, step).wait_recv()
                    if once(way, step + 1, hz):
                        i_copy(way, step + 1).start()
                    if step < hy:
                        j_copy(way, step).wait_recv()
                        if once(way, step + 1, hy):
                            j_copy(way, step + 1).start()
            if not some_base(3):
                some_units(4)
            if step == hy and c == 2:
                early_up()
    while state["w"] < len(w_waits):
        next_w()
    some_base(nt)

    def p_copy(g):
        span = pl.ds(groups[g][0], groups[g][1] - groups[g][0])
        return remote(
            acc.at[span, 1 - core], halves.at[span], p_send.at[g], p_recv.at[g], r, t + 1 - 2 * core
        )

    def a_copy(i, g):
        to = (x + i) % nx
        span = pl.ds(groups[g][0], groups[g][1] - groups[g][0])
        return remote(
            part.at[span, to], rs.at[i, span], a_send.at[g, i], a_recv.at[g, i], r, 2 * to + core
        )

    def pass_on(g):
        low, high = groups[g]
        p_copy(g).wait_recv()
        part[low:high] = acc[low:high, core] + halves[low:high]
        lax.fori_loop(1, nx, lambda i, _: (a_copy(i, g).start(), 0)[1], 0)

    def l_copy(i):
        to = (t + i) % nt
        return remote(acc.at[nz - 1, to % 2, to // 2], lasts.at[i], l_send.at[i], l_recv.at[i], r, to)

    def finish_a(g):
        low, high = groups[g]
        if g == last:
            lax.fori_loop(1, nt, lambda i, _: (l_copy(i).wait_recv(), 0)[1], 0)
            total = acc[nz - 1, core, x]
            for i in range(1, nt):
                total = total + lasts[i]
            sh[nz - 1] = total.astype(BF16)
            return
        lax.fori_loop(1, nx, lambda i, _: (a_copy(i, g).wait_recv(), 0)[1], 0)
        total = part[low:high, x]
        for i in range(1, nx):
            total = total + rs[i, low:high]
        sh[low:high] = total.astype(BF16)

    def b_copy(k):
        d = 0 if k == 0 else next(d for d in range(1, nz) if slot_of(d, nz) == k)
        return remote(
            sh.at[k], hm.at[slot_of(-d, nz)], b_send.at[k], b_recv.at[slot_of(-d, nz)], at_z(d), t
        )

    def finish(g):
        low, high = groups[g]
        finish_a(g)
        for k in range(low, high):
            if k == 0:
                hm[0] = sh[0]
            else:
                b_copy(k).start()

    def rest_of(g):
        low, high = groups[g]
        for k in range(low, high):
            ms = [m for m in range(ny) if (k, m) in pending]
            mates = [n for n in range(k, high) if [m for m in range(ny) if (n, m) in pending] == ms]
            if ms and mates == list(range(k, k + len(mates))) and ms == list(range(ms[0], ny)):
                units(k, k + len(mates), ms[0], ny)
                pending.difference_update((n, m) for n in mates for m in ms)
            else:
                for m in ms:
                    units(k, k + 1, m, m + 1)
                    pending.discard((k, m))
        if g < last:
            p_copy(g).start()
        else:
            lax.fori_loop(1, nt, lambda i, _: (l_copy(i).start(), 0)[1], 0)

    def u_pass(step):
        for h in range(2):
            for way in range(2):
                if u_takes(way, step, h):
                    u_copy(way, step, h).wait_recv()
                    if u_takes(way, step + 1, h):
                        u_copy(way, step + 1, h).start()

    def s_finish(g):
        for d in range(1, ny):
            s_copy(d, g).wait_recv()
            spread_up(ny - d, g)

    for step in range(hz, hy):
        for way in range(2):
            j_copy(way, step).wait_recv()
            if once(way, step + 1, hy):
                j_copy(way, step + 1).start()
    early_up()
    for g in range(last):
        rest_of(g)
        if g:
            pass_on(g - 1)
    for c in range(CHUNKS // 2):
        z_copy(0, hz, c).wait_recv()
        z_copy(1, hz, c + CHUNKS // 2).wait_recv()
        if c == 0:
            u_pass(1)
            pass_on(last - 1)
    i_copy(0, hz).wait_recv()
    wide_column(nz - 1, idz[nz - 1])
    rest_of(last)
    for g in range(last):
        finish(g)
    u_group(1)
    if hz > 1:
        u_pass(2)
    finish(last)
    if hz > 1:
        u_group(2)
    for step in range(3, hz):
        u_pass(step)
        u_group(step)

    for k in range(1, nz):
        b_copy(k).wait_recv()
    mine = hm[0].astype(F32)
    for k in range(1, nz):
        mine = mine + hm[k].astype(F32)
    sr[share] = mine.astype(BF16)

    def c_copy(i):
        return remote(sr.at[share], sr.at[share], c_send.at[i], c_recv.at[i], r, (t + i) % nt)

    def c_arrival(i):
        src = (t + nt - i) % nt
        at = (src % 2) * nx + src // 2
        return remote(sr.at[at], sr.at[at], c_send.at[i], c_recv.at[i], r, src)

    lax.fori_loop(1, nt, lambda i, _: (c_copy(i).start(), 0)[1], 0)
    if hz > 2:
        u_pass(hz)
        u_group(hz)
    for g in range(hz + 1):
        s_finish(g)
    lax.fori_loop(1, nt, lambda i, _: (c_arrival(i).wait_recv(), 0)[1], 0)

    shrink = sr[...].astype(F32).reshape(rows, rank)
    wanted = colbuf[0]

    total = base[...]
    for e in range(ny):
        parts = []
        for k in range(nz):
            first = (((z + shift_of(k, nz)) % nz) * ny + (y + e) % ny) * adapters
            uses_it = (wanted >= first) & (wanted < first + adapters)
            parts.append(jnp.where(uses_it, shrink, 0.0).astype(BF16))
        spread = jnp.concatenate(parts, axis=1)
        total = total + SCALE * jnp.dot(spread, bd[e], preferred_element_type=F32)
    projected = total.astype(BF16)
    stacked = jnp.concatenate([projected[:, 0:128], projected[:, 128:256]], axis=0)
    cache = jnp.dot(perm[...], stacked, preferred_element_type=F32).astype(BF16)
    kvs[...] = cache.reshape(replicas, cap2, 128)

    def o_copy(i):
        to = ((z + shift_of(i // ny, nz)) % nz) * ny + (y + i % ny) % ny
        return remote(
            kvs.at[to], out.at[pl.ds(pl.multiple_of(r * cap2, cap2), cap2)],
            o_send.at[i], o_recv.at[i], to, t,
        )

    def o_arrival(i):
        src = ((z + nz - shift_of(i // ny, nz)) % nz) * ny + (y + ny - i % ny) % ny
        return remote(
            kvs.at[src], out.at[pl.ds(pl.multiple_of(src * cap2, cap2), cap2)],
            o_send.at[i], o_recv.at[i], src, t,
        )

    lax.fori_loop(1, replicas, lambda i, _: (o_copy(replicas - i).start(), 0)[1], 0)
    own_o = pltpu.make_async_copy(
        kvs.at[r], out.at[pl.ds(pl.multiple_of(r * cap2, cap2), cap2)], local_sem.at[4 + nt]
    )
    own_o.start()

    for way in range(2):
        for step in range(1, hz + 1):
            for c in range(CHUNKS):
                if z_takes(way, step, c):
                    z_copy(way, step, c).wait_send()
            if once(way, step, hz):
                i_copy(way, step).wait_send()
            for h in range(2):
                if u_takes(way, step, h):
                    u_copy(way, step, h).wait_send()
        for step in range(1, hy + 1):
            for j in range(adapters):
                if w_takes(way, step, j):
                    w_copy(way, step, j).wait_send()
            if once(way, step, hy):
                j_copy(way, step).wait_send()
    for d in range(1, ny):
        for g in range(hz + 1):
            s_copy(d, g).wait_send()
    for k in range(1, nz):
        b_copy(k).wait_send()

    def tensor_sends(i, _):
        c_copy(i).wait_send()
        l_copy(i).wait_send()
        return 0

    lax.fori_loop(1, nt, tensor_sends, 0)
    for g in range(last):
        p_copy(g).wait_send()
        lax.fori_loop(1, nx, lambda i, _, g=g: (a_copy(i, g).wait_send(), 0)[1], 0)

    def cache_rows(i, _):
        o_copy(i).wait_send()
        o_arrival(i).wait_recv()
        return 0

    lax.fori_loop(1, replicas, cache_rows, 0)
    own_o.wait()


def shards(nz, hidden, key_value_weight, adapter_down_weight, adapter_up_weight, token_adapter_index, destinations):
    replicas = lax.axis_size("replica")
    nt = lax.axis_size("tensor")
    ny = replicas // nz
    rows, model = hidden.shape
    width = model // nt
    adapters, _, rank = adapter_down_weight.shape
    cols = key_value_weight.shape[2]
    cap2 = 2 * (2 * rows // replicas)
    sub = rows // nt
    hz, hy = nz // 2, ny // 2
    vm = pltpu.VMEM
    dma = pltpu.SemaphoreType.DMA
    scratch = [
        vm((nt, rows, width), BF16),
        vm((2 * model, cols), BF16),
        vm((2 * width, cols), F32),
        vm((rows, 2 * cols), F32),
        vm((nz, rows, width), BF16),
        vm((ny, adapters, width, rank), BF16),
        vm((nz, adapters * rank, cols), BF16),
        vm((nz, rows, rank), jnp.int32),
        vm((nz, 1, rows), jnp.int32),
        vm((ny, 1, rows), jnp.int32),
        vm((nz, 2, nt // 2, sub, rank), F32),
        vm((nz, nt // 2, sub, rank), F32),
        vm((nz, nt // 2, sub, rank), F32),
        vm((nt // 2, nz, sub, rank), F32),
        vm((nt, sub, rank), F32),
        vm((nz, sub, rank), BF16),
        vm((nz, sub, rank), BF16),
        vm((nt, sub, rank), BF16),
        vm((ny, nz * adapters, 128), F32),
        vm((ny, nz, rank, cols), BF16),
        vm((ny, nz, rank, cols), BF16),
        vm((ny, nz * rank, 2 * cols), BF16),
        vm((replicas * cap2, 2 * rows), BF16),
        vm((replicas, cap2, cols), BF16),
        dma((5 + nt,)),
        dma((2, hz + 1, CHUNKS)), dma((2, hz + 1, CHUNKS)),
        dma((2, hy + 1, adapters)), dma((2, hy + 1, adapters)),
        dma((2, hz + 1, 2)), dma((2, hz + 1, 2)),
        dma((2, hz + 1)), dma((2, hz + 1)),
        dma((2, hy + 1)), dma((2, hy + 1)),
        dma((nt,)), dma((nt,)),
        dma((hz + 1,)), dma((hz + 1,)),
        dma((hz + 1, nt)), dma((hz + 1, nt)),
        dma((nz,)), dma((nz,)),
        dma((nt,)), dma((nt,)),
        dma((ny, hz + 1)), dma((ny, hz + 1)),
        dma((replicas,)), dma((replicas,)),
    ]
    hbm = pl.BlockSpec(memory_space=pltpu.HBM)
    in_vmem = pl.BlockSpec(memory_space=pltpu.VMEM)
    cache = pl.pallas_call(
        functools.partial(kernel, (nz, ny, nt)),
        out_shape=pltpu.VMEM((replicas * cap2, cols), BF16),
        in_specs=[hbm, hbm, hbm, hbm, in_vmem, in_vmem],
        out_specs=in_vmem,
        scratch_shapes=scratch,
        compiler_params=pltpu.CompilerParams(
            collective_id=0, has_side_effects=True, vmem_limit_bytes=56 * 1024 * 1024
        ),
        cost_estimate=pl.CostEstimate(
            flops=2 * rows * model * 2 * cols + 2 * nz * rows * width * ny * adapters * rank,
            bytes_accessed=2 * (rows * model + 2 * model * cols + adapters * width * rank),
            transcendentals=0,
        ),
    )(
        hidden,
        key_value_weight.reshape(2 * model, cols),
        adapter_down_weight,
        adapter_up_weight.reshape(adapters * rank, cols),
        token_adapter_index.reshape(1, rows),
        destinations.reshape(1, rows),
    )
    return cache.reshape(replicas * cap2 // 2, 2, cols)


def solution(mesh):
    placed = (
        P("replica", None),
        P(None, None, "tensor"),
        P("replica", "tensor", None),
        P("replica", None, None, "tensor"),
        P("replica"),
        P("replica", None),
    )
    return jax.shard_map(
        functools.partial(shards, RINGS), mesh=mesh, in_specs=placed,
        out_specs=P("replica", None, "tensor"), check_vma=False,
    )
```

```python
import functools

import jax
import jax.numpy as jnp
from jax import lax
from jax.experimental import pallas as pl
from jax.experimental.pallas import tpu as pltpu
from jax.sharding import PartitionSpec as P

RINGS = 8
USE = 8
SCALE = 0.5
CHUNKS = 4

BF16 = jnp.bfloat16
F32 = jnp.float32
MESH = pl.DeviceIdType.MESH


def slot_of(d, n):
    d %= n
    return 0 if d == 0 else (2 * d - 1 if d <= n // 2 else 2 * (n - d))


def shift_of(k, n):
    odd = k % 2
    return odd * ((k + 1) // 2) + (1 - odd) * ((n - k // 2) % n)


def kernel(
    dims,
    hid, kvw, down, up, idx, dest,
    out,
    hf, kvb, kvf, base, hbuf, wbuf, upz, colbuf, idz, idy, acc, halves, part, rs, lasts, sh, hm, sr, uses, upsend, upsel, bd, perm, kvs,
    local_sem, z_send, z_recv, w_send, w_recv, u_send, u_recv, i_send, i_recv, j_send, j_recv,
    l_send, l_recv, p_send, p_recv, a_send, a_recv, b_send, b_recv, c_send, c_recv, s_send, s_recv, o_send, o_recv,
):
    nz, ny, nt = dims
    rows, width = hbuf.shape[1], hbuf.shape[2]
    adapters, rank = wbuf.shape[1], wbuf.shape[3]
    sub = rows // nt
    piece = rows // CHUNKS
    cap2 = kvs.shape[1]
    replicas = nz * ny
    hz, hy = nz // 2, ny // 2

    r = lax.axis_index("replica")
    t = lax.axis_index("tensor")
    z, y = r // ny, r % ny
    nx = nt // 2
    x, core = t // 2, t % 2
    share = core * nx + x

    def at_z(d):
        return ((z + d + nz) % nz) * ny + y

    def at_y(d):
        return z * ny + (y + d + ny) % ny

    def remote(src, dst, send, recv, replica, tensor):
        return pltpu.make_async_remote_copy(
            src_ref=src, dst_ref=dst, send_sem=send, recv_sem=recv,
            device_id=(replica, tensor), device_id_type=MESH,
        )

    barrier = pltpu.get_barrier_semaphore()

    def greet_tensor(i, _):
        pl.semaphore_signal(barrier, inc=1, device_id=(r, (t + i) % nt), device_id_type=MESH)
        return 0

    for to in (at_z(1), at_z(-1), at_y(1), at_y(-1)):
        pl.semaphore_signal(barrier, inc=1, device_id=(to, t), device_id_type=MESH)
    lax.fori_loop(1, nt, greet_tensor, 0)

    own_cols = pl.ds(pl.multiple_of(t * width, 128), width)
    own_h = pltpu.make_async_copy(hid.at[:, own_cols], hbuf.at[0], local_sem.at[0])
    own_w = pltpu.make_async_copy(down, wbuf.at[0], local_sem.at[1])
    own_u = pltpu.make_async_copy(up, upz.at[0], local_sem.at[2])
    own_k = pltpu.make_async_copy(kvw, kvb, local_sem.at[3])

    def full_copy(c):
        return pltpu.make_async_copy(
            hid.at[:, pl.ds(pl.multiple_of(c * width, 128), width)], hf.at[c], local_sem.at[4 + c]
        )

    own_h.start()
    own_w.start()
    own_u.start()
    own_k.start()
    lax.fori_loop(0, nt, lambda c, _: (full_copy(c).start(), 0)[1], 0)

    pl.semaphore_wait(barrier, 4 + nt - 1)

    def z_copy(way, step, c):
        part = pl.ds(c * piece, piece)
        sign = -1 if way == 0 else 1
        to = at_z(1 if way == 0 else -1)
        dst = hbuf.at[slot_of(sign * step, nz), part]
        if step == 1:
            src = hid.at[part, own_cols]
        else:
            src = hbuf.at[slot_of(sign * (step - 1), nz), part]
        return remote(src, dst, z_send.at[way, step, c], z_recv.at[way, step, c], to, t)

    def z_takes(way, step, c):
        return step < hz or (step == hz and (c < CHUNKS // 2) == (way == 0))

    def u_copy(way, step, h):
        sign = -1 if way == 0 else 1
        to = at_z(1 if way == 0 else -1)
        n = upz.shape[1] // 2
        part = pl.ds(h * n, n)
        dst = upz.at[slot_of(sign * step, nz), part]
        if step == 1:
            src = up.at[part]
        else:
            src = upz.at[slot_of(sign * (step - 1), nz), part]
        return remote(src, dst, u_send.at[way, step, h], u_recv.at[way, step, h], to, t)

    def u_takes(way, step, h):
        return step < hz or (step == hz and h == way)

    def u_start():
        for h in range(2):
            for way in range(2):
                if u_takes(way, 1, h):
                    u_copy(way, 1, h).start()

    def w_copy(way, step, j):
        sign = -1 if way == 0 else 1
        to = at_y(1 if way == 0 else -1)
        dst = wbuf.at[slot_of(sign * step, ny), j]
        src = down.at[j] if step == 1 else wbuf.at[slot_of(sign * (step - 1), ny), j]
        return remote(src, dst, w_send.at[way, step, j], w_recv.at[way, step, j], to, t)

    def w_takes(way, step, j):
        return step < hy or (step == hy and (j < adapters // 2) == (way == 0))

    def i_copy(way, step):
        sign = -1 if way == 0 else 1
        src = idx if step == 1 else idz.at[slot_of(sign * (step - 1), nz)]
        dst = idz.at[slot_of(sign * step, nz)]
        to = at_z(1 if way == 0 else -1)
        return remote(src, dst, i_send.at[way, step], i_recv.at[way, step], to, t)

    def j_copy(way, step):
        sign = -1 if way == 0 else 1
        src = idx if step == 1 else idy.at[(sign * (step - 1)) % ny]
        dst = idy.at[(sign * step) % ny]
        to = at_y(1 if way == 0 else -1)
        return remote(src, dst, j_send.at[way, step], j_recv.at[way, step], to, t)

    def once(way, step, half_way):
        return step < half_way or (step == half_way and way == 0)

    for way in range(2):
        if once(way, 1, hz):
            i_copy(way, 1).start()
        if once(way, 1, hy):
            j_copy(way, 1).start()
    w_order = [list(range(adapters)), list(range(adapters // 2, adapters)) + list(range(adapters // 2))]
    for c in range(CHUNKS):
        for way in range(2):
            if z_takes(way, 1, c):
                z_copy(way, 1, c).start()
        for way in range(2):
            if c < adapters and w_takes(way, 1, w_order[way][c]):
                w_copy(way, 1, w_order[way][c]).start()
    u_start()

    eye = lax.broadcasted_iota(jnp.int32, (rows, rows), 0) == lax.broadcasted_iota(
        jnp.int32, (rows, rows), 1
    )

    def column(row):
        wide = jnp.broadcast_to(row, (rows, rows))
        return jnp.sum(jnp.where(eye, wide, 0.0), axis=1, keepdims=True)

    def base_part(c, _):
        words = 2 * width
        at = pl.ds(pl.multiple_of(c * words, 128), words)
        kvf[...] = kvb[at, :].astype(F32)
        keys = kvf[pl.ds(0, width, stride=2), :].astype(BF16)
        values = kvf[pl.ds(1, width, stride=2), :].astype(BF16)
        both = jnp.concatenate([keys, values], axis=1)
        base[...] += jnp.dot(hf[c], both, preferred_element_type=F32)
        return 0

    def unit(k, m):
        mate = shift_of(m, ny)
        first = (z * ny + (y + mate) % ny) * adapters
        wanted = colbuf[k]
        total = acc[k].reshape(rows, rank)
        h = hbuf[k]
        for pair in range(adapters // 2):
            w = jnp.concatenate([wbuf[m, 2 * pair], wbuf[m, 2 * pair + 1]], axis=1)
            got = jnp.dot(h, w, preferred_element_type=F32)
            for j in range(2):
                mine = wanted == first + 2 * pair + j
                total = total + jnp.where(mine, got[:, j * rank : (j + 1) * rank], 0.0)
        acc[k] = total.reshape(2, nx, sub, rank)

    def units(k_low, k_high, m_low, m_high):
        count = m_high - m_low

        def one(i, _):
            unit(k_low + i // count, m_low + i % count)
            return 0

        if (k_high - k_low) * count == 1:
            unit(k_low, m_low)
        else:
            lax.fori_loop(0, (k_high - k_low) * count, one, 0)

    base[...] = jnp.zeros_like(base)
    acc[...] = jnp.zeros_like(acc)
    to_row = dest[...].astype(F32)
    to_col = column(to_row)
    before = lax.broadcasted_iota(jnp.int32, (rows, rows), 0) < lax.broadcasted_iota(
        jnp.int32, (rows, rows), 1
    )
    earlier = jnp.where(before & (to_col == to_row), 1.0, 0.0)
    order = jnp.sum(earlier, axis=0, keepdims=True)
    place = to_row * float(cap2) + order * 2.0
    n_perm = perm.shape[0]
    for p in range(2):
        target = lax.broadcasted_iota(jnp.int32, (n_perm, rows), 0).astype(F32)
        perm[:, p * rows : (p + 1) * rows] = jnp.where(target == place + float(p), 1.0, 0.0).astype(
            BF16
        )

    def wide_column(k, row):
        colbuf[k] = jnp.broadcast_to(column(row.astype(F32)), (rows, rank)).astype(jnp.int32)

    wide_column(0, idx[...])
    own_h.wait()
    own_w.wait()
    own_k.wait()
    lax.fori_loop(0, nt, lambda c, _: (full_copy(c).wait(), 0)[1], 0)

    last = hz
    groups = [(0, 1)] + [(2 * s - 1, 2 * s + 1) for s in range(1, hz)] + [(nz - 1, nz)]
    state = {"base": 0, "w": 0, "up": 0}
    here_k, here_m = {0}, {0}
    pending = {(k, m) for k in range(nz) for m in range(ny)}
    w_waits = [
        [(way, 1, w_order[way][n]) for way in range(2) if w_takes(way, 1, w_order[way][n])]
        for n in range(adapters)
    ]
    if hy > 1:
        half = adapters // 2
        w_waits += [[(way, 2, w_order[way][n]) for way in range(2)] for n in range(half)]
    w_waits = [pair for pair in w_waits if pair]

    def mark_uses(e, wanted):
        count = nz * adapters
        row = lax.broadcasted_iota(jnp.int32, (count, rows), 0)
        number = jnp.zeros((count, rows), jnp.int32)
        for k in range(nz):
            first = (((z + shift_of(k, nz)) % nz) * ny + y) * adapters
            here = (row >= k * adapters) & (row < (k + 1) * adapters)
            number = jnp.where(here, first + row - k * adapters, number)
        found = jnp.where(number == jnp.broadcast_to(wanted, (count, rows)), 1.0, 0.0)
        uses[e] = jnp.broadcast_to(jnp.max(found, axis=1, keepdims=True), (count, 128))

    def select_up(e, into, low, high):
        for k in range(low, high):
            total = jnp.zeros((rank, 128), F32)
            for j in range(adapters):
                at = k * adapters + j
                total = total + uses[e, at : at + 1] * upz[k, j * rank : (j + 1) * rank].astype(F32)
            into[k] = total.astype(BF16)

    u_groups = groups

    def s_copy(d, g):
        span = pl.ds(u_groups[g][0], u_groups[g][1] - u_groups[g][0])
        return remote(
            upsend.at[d, span], upsel.at[(-d) % ny, span], s_send.at[d, g], s_recv.at[d, g], at_y(d), t
        )

    rank_half = (lax.broadcasted_iota(jnp.int32, (rank, 128), 0) < rank // 2).astype(F32)

    def spread_up(e, g):
        def one(k, _):
            block = upsel[e, k].astype(F32)
            at = pl.ds(pl.multiple_of(k * rank, rank), rank)
            bd[e, at, 0:128] = (block * rank_half).astype(BF16)
            bd[e, at, 128:256] = (block * (1.0 - rank_half)).astype(BF16)
            return 0

        lax.fori_loop(u_groups[g][0], u_groups[g][1], one, 0)

    def u_group(g):
        for d in range(1, ny):
            select_up(d, upsend.at[d], *u_groups[g])
            s_copy(d, g).start()
        select_up(0, upsel.at[0], *u_groups[g])
        spread_up(0, g)

    def early_up():
        if state["up"]:
            return
        state["up"] = 1
        j_copy(0, hy).wait_recv()
        own_u.wait()
        mark_uses(0, idx[...])
        for d in range(1, ny):
            mark_uses(d, idy[d])
        u_group(0)

    def some_units(budget):
        while budget > 0:
            ready = sorted((m, k) for k, m in pending if k in here_k and m in here_m)
            if not ready:
                return
            m, low = ready[0]
            high = low
            while (m, high) in ready and high - low < budget:
                pending.discard((high, m))
                high += 1
            units(low, high, m, m + 1)
            budget -= high - low

    def next_w():
        if state["w"] == len(w_waits):
            return
        for way, step, j in w_waits[state["w"]]:
            w_copy(way, step, j).wait_recv()
            if step < hy and w_takes(way, step + 1, j):
                w_copy(way, step + 1, j).start()
        state["w"] += 1
        if state["w"] == len(w_waits):
            here_m.update(range(ny))
        elif hy > 1 and state["w"] == adapters:
            here_m.update((1, 2))

    def some_base(count):
        low = state["base"]
        high = min(nt, low + count)
        if low < high:
            lax.fori_loop(low, high, base_part, 0)
        state["base"] = high
        return high - low

    for step in range(1, hz):
        for c in range(CHUNKS):
            for way in range(2):
                z_copy(way, step, c).wait_recv()
                if z_takes(way, step + 1, c):
                    z_copy(way, step + 1, c).start()
            if c % 2 == 1:
                next_w()
            if c == CHUNKS - 1:
                for way in range(2):
                    k = slot_of(-step if way == 0 else step, nz)
                    wide_column(k, idz[k])
                    here_k.add(k)
            if c == 0:
                for way in range(2):
                    i_copy(way, step).wait_recv()
                    if once(way, step + 1, hz):
                        i_copy(way, step + 1).start()
                    if step < hy:
                        j_copy(way, step).wait_recv()
                        if once(way, step + 1, hy):
                            j_copy(way, step + 1).start()
            if not some_base(3):
                some_units(4)
            if step == hy and c == 2:
                early_up()
    while state["w"] < len(w_waits):
        next_w()
    some_base(nt)

    def p_copy(g):
        span = pl.ds(groups[g][0], groups[g][1] - groups[g][0])
        return remote(
            acc.at[span, 1 - core], halves.at[span], p_send.at[g], p_recv.at[g], r, t + 1 - 2 * core
        )

    def a_copy(i, g):
        to = (x + i) % nx
        span = pl.ds(groups[g][0], groups[g][1] - groups[g][0])
        return remote(
            part.at[span, to], rs.at[i, span], a_send.at[g, i], a_recv.at[g, i], r, 2 * to + core
        )

    def pass_on(g):
        low, high = groups[g]
        p_copy(g).wait_recv()
        part[low:high] = acc[low:high, core] + halves[low:high]
        lax.fori_loop(1, nx, lambda i, _: (a_copy(i, g).start(), 0)[1], 0)

    def l_copy(i):
        to = (t + i) % nt
        return remote(acc.at[nz - 1, to % 2, to // 2], lasts.at[i], l_send.at[i], l_recv.at[i], r, to)

    def finish_a(g):
        low, high = groups[g]
        if g == last:
            lax.fori_loop(1, nt, lambda i, _: (l_copy(i).wait_recv(), 0)[1], 0)
            total = acc[nz - 1, core, x]
            for i in range(1, nt):
                total = total + lasts[i]
            sh[nz - 1] = total.astype(BF16)
            return
        lax.fori_loop(1, nx, lambda i, _: (a_copy(i, g).wait_recv(), 0)[1], 0)
        total = part[low:high, x]
        for i in range(1, nx):
            total = total + rs[i, low:high]
        sh[low:high] = total.astype(BF16)

    def b_copy(k):
        d = 0 if k == 0 else next(d for d in range(1, nz) if slot_of(d, nz) == k)
        return remote(
            sh.at[k], hm.at[slot_of(-d, nz)], b_send.at[k], b_recv.at[slot_of(-d, nz)], at_z(d), t
        )

    def finish(g):
        low, high = groups[g]
        finish_a(g)
        for k in range(low, high):
            if k == 0:
                hm[0] = sh[0]
            else:
                b_copy(k).start()

    def rest_of(g):
        low, high = groups[g]
        for k in range(low, high):
            ms = [m for m in range(ny) if (k, m) in pending]
            mates = [n for n in range(k, high) if [m for m in range(ny) if (n, m) in pending] == ms]
            if ms and mates == list(range(k, k + len(mates))) and ms == list(range(ms[0], ny)):
                units(k, k + len(mates), ms[0], ny)
                pending.difference_update((n, m) for n in mates for m in ms)
            else:
                for m in ms:
                    units(k, k + 1, m, m + 1)
                    pending.discard((k, m))
        if g < last:
            p_copy(g).start()
        else:
            lax.fori_loop(1, nt, lambda i, _: (l_copy(i).start(), 0)[1], 0)

    def u_pass(step):
        for h in range(2):
            for way in range(2):
                if u_takes(way, step, h):
                    u_copy(way, step, h).wait_recv()
                    if u_takes(way, step + 1, h):
                        u_copy(way, step + 1, h).start()

    def s_finish(g):
        for d in range(1, ny):
            s_copy(d, g).wait_recv()
            spread_up(ny - d, g)

    for step in range(hz, hy):
        for way in range(2):
            j_copy(way, step).wait_recv()
            if once(way, step + 1, hy):
                j_copy(way, step + 1).start()
    early_up()
    for g in range(last):
        rest_of(g)
        if g:
            pass_on(g - 1)
    for c in range(CHUNKS // 2):
        z_copy(0, hz, c).wait_recv()
        z_copy(1, hz, c + CHUNKS // 2).wait_recv()
        if c == 0:
            u_pass(1)
            pass_on(last - 1)
    i_copy(0, hz).wait_recv()
    wide_column(nz - 1, idz[nz - 1])
    rest_of(last)
    for g in range(last):
        finish(g)
    u_group(1)
    if hz > 1:
        u_pass(2)
    finish(last)
    if hz > 1:
        u_group(2)
    for step in range(3, hz):
        u_pass(step)
        u_group(step)
        s_finish(step - 3)
        s_finish(step - 2)

    for k in range(1, nz):
        b_copy(k).wait_recv()
    mine = hm[0].astype(F32)
    for k in range(1, nz):
        mine = mine + hm[k].astype(F32)
    sr[share] = mine.astype(BF16)

    def c_copy(i):
        return remote(sr.at[share], sr.at[share], c_send.at[i], c_recv.at[i], r, (t + i) % nt)

    def c_arrival(i):
        src = (t + nt - i) % nt
        at = (src % 2) * nx + src // 2
        return remote(sr.at[at], sr.at[at], c_send.at[i], c_recv.at[i], r, src)

    lax.fori_loop(1, nt, lambda i, _: (c_copy(i).start(), 0)[1], 0)
    if hz > 2:
        u_pass(hz)
        u_group(hz)
    for g in range(2 if hz > 3 else 0, hz + 1):
        s_finish(g)
    lax.fori_loop(1, nt, lambda i, _: (c_arrival(i).wait_recv(), 0)[1], 0)

    shrink = sr[...].astype(F32).reshape(rows, rank)
    wanted = colbuf[0]

    total = base[...]
    for e in range(ny):
        parts = []
        for k in range(nz):
            first = (((z + shift_of(k, nz)) % nz) * ny + (y + e) % ny) * adapters
            uses_it = (wanted >= first) & (wanted < first + adapters)
            parts.append(jnp.where(uses_it, shrink, 0.0).astype(BF16))
        spread = jnp.concatenate(parts, axis=1)
        total = total + SCALE * jnp.dot(spread, bd[e], preferred_element_type=F32)
    projected = total.astype(BF16)
    stacked = jnp.concatenate([projected[:, 0:128], projected[:, 128:256]], axis=0)
    cache = jnp.dot(perm[...], stacked, preferred_element_type=F32).astype(BF16)
    kvs[...] = cache.reshape(replicas, cap2, 128)

    def o_copy(i):
        to = ((z + shift_of(i // ny, nz)) % nz) * ny + (y + i % ny) % ny
        return remote(
            kvs.at[to], out.at[pl.ds(pl.multiple_of(r * cap2, cap2), cap2)],
            o_send.at[i], o_recv.at[i], to, t,
        )

    def o_arrival(i):
        src = ((z + nz - shift_of(i // ny, nz)) % nz) * ny + (y + ny - i % ny) % ny
        return remote(
            kvs.at[src], out.at[pl.ds(pl.multiple_of(src * cap2, cap2), cap2)],
            o_send.at[i], o_recv.at[i], src, t,
        )

    lax.fori_loop(1, replicas, lambda i, _: (o_copy(replicas - i).start(), 0)[1], 0)
    own_o = pltpu.make_async_copy(
        kvs.at[r], out.at[pl.ds(pl.multiple_of(r * cap2, cap2), cap2)], local_sem.at[4 + nt]
    )
    own_o.start()

    for way in range(2):
        for step in range(1, hz + 1):
            for c in range(CHUNKS):
                if z_takes(way, step, c):
                    z_copy(way, step, c).wait_send()
            if once(way, step, hz):
                i_copy(way, step).wait_send()
            for h in range(2):
                if u_takes(way, step, h):
                    u_copy(way, step, h).wait_send()
        for step in range(1, hy + 1):
            for j in range(adapters):
                if w_takes(way, step, j):
                    w_copy(way, step, j).wait_send()
            if once(way, step, hy):
                j_copy(way, step).wait_send()
    for d in range(1, ny):
        for g in range(hz + 1):
            s_copy(d, g).wait_send()
    for k in range(1, nz):
        b_copy(k).wait_send()

    def tensor_sends(i, _):
        c_copy(i).wait_send()
        l_copy(i).wait_send()
        return 0

    lax.fori_loop(1, nt, tensor_sends, 0)
    for g in range(last):
        p_copy(g).wait_send()
        lax.fori_loop(1, nx, lambda i, _, g=g: (a_copy(i, g).wait_send(), 0)[1], 0)

    def cache_rows(i, _):
        o_copy(i).wait_send()
        o_arrival(i).wait_recv()
        return 0

    lax.fori_loop(1, replicas, cache_rows, 0)
    own_o.wait()


def shards(nz, hidden, key_value_weight, adapter_down_weight, adapter_up_weight, token_adapter_index, destinations):
    replicas = lax.axis_size("replica")
    nt = lax.axis_size("tensor")
    ny = replicas // nz
    rows, model = hidden.shape
    width = model // nt
    adapters, _, rank = adapter_down_weight.shape
    cols = key_value_weight.shape[2]
    cap2 = 2 * (2 * rows // replicas)
    sub = rows // nt
    hz, hy = nz // 2, ny // 2
    vm = pltpu.VMEM
    dma = pltpu.SemaphoreType.DMA
    scratch = [
        vm((nt, rows, width), BF16),
        vm((2 * model, cols), BF16),
        vm((2 * width, cols), F32),
        vm((rows, 2 * cols), F32),
        vm((nz, rows, width), BF16),
        vm((ny, adapters, width, rank), BF16),
        vm((nz, adapters * rank, cols), BF16),
        vm((nz, rows, rank), jnp.int32),
        vm((nz, 1, rows), jnp.int32),
        vm((ny, 1, rows), jnp.int32),
        vm((nz, 2, nt // 2, sub, rank), F32),
        vm((nz, nt // 2, sub, rank), F32),
        vm((nz, nt // 2, sub, rank), F32),
        vm((nt // 2, nz, sub, rank), F32),
        vm((nt, sub, rank), F32),
        vm((nz, sub, rank), BF16),
        vm((nz, sub, rank), BF16),
        vm((nt, sub, rank), BF16),
        vm((ny, nz * adapters, 128), F32),
        vm((ny, nz, rank, cols), BF16),
        vm((ny, nz, rank, cols), BF16),
        vm((ny, nz * rank, 2 * cols), BF16),
        vm((replicas * cap2, 2 * rows), BF16),
        vm((replicas, cap2, cols), BF16),
        dma((5 + nt,)),
        dma((2, hz + 1, CHUNKS)), dma((2, hz + 1, CHUNKS)),
        dma((2, hy + 1, adapters)), dma((2, hy + 1, adapters)),
        dma((2, hz + 1, 2)), dma((2, hz + 1, 2)),
        dma((2, hz + 1)), dma((2, hz + 1)),
        dma((2, hy + 1)), dma((2, hy + 1)),
        dma((nt,)), dma((nt,)),
        dma((hz + 1,)), dma((hz + 1,)),
        dma((hz + 1, nt)), dma((hz + 1, nt)),
        dma((nz,)), dma((nz,)),
        dma((nt,)), dma((nt,)),
        dma((ny, hz + 1)), dma((ny, hz + 1)),
        dma((replicas,)), dma((replicas,)),
    ]
    hbm = pl.BlockSpec(memory_space=pltpu.HBM)
    in_vmem = pl.BlockSpec(memory_space=pltpu.VMEM)
    cache = pl.pallas_call(
        functools.partial(kernel, (nz, ny, nt)),
        out_shape=pltpu.VMEM((replicas * cap2, cols), BF16),
        in_specs=[hbm, hbm, hbm, hbm, in_vmem, in_vmem],
        out_specs=in_vmem,
        scratch_shapes=scratch,
        compiler_params=pltpu.CompilerParams(
            collective_id=0, has_side_effects=True, vmem_limit_bytes=56 * 1024 * 1024
        ),
        cost_estimate=pl.CostEstimate(
            flops=2 * rows * model * 2 * cols + 2 * nz * rows * width * ny * adapters * rank,
            bytes_accessed=2 * (rows * model + 2 * model * cols + adapters * width * rank),
            transcendentals=0,
        ),
    )(
        hidden,
        key_value_weight.reshape(2 * model, cols),
        adapter_down_weight,
        adapter_up_weight.reshape(adapters * rank, cols),
        token_adapter_index.reshape(1, rows),
        destinations.reshape(1, rows),
    )
    return cache.reshape(replicas * cap2 // 2, 2, cols)


def solution(mesh):
    placed = (
        P("replica", None),
        P(None, None, "tensor"),
        P("replica", "tensor", None),
        P("replica", None, None, "tensor"),
        P("replica"),
        P("replica", None),
    )
    return jax.shard_map(
        functools.partial(shards, RINGS), mesh=mesh, in_specs=placed,
        out_specs=P("replica", None, "tensor"), check_vma=False,
    )
```
